256 devices in a mesh: expert: 32 (over z, x), dp: 8 (over y, core).
Axes of the slice: x: 4, y: 4, z: 8, core: 2. Of those that a mesh axis runs over, the one named last changes fastest.
Arguments:
- tokens: bfloat16 [3072, 4096], P('expert', 'dp'), may hold values from -6 to 6
- route_weight: float32 [3072, 8], P('expert'), may hold values from 0.05 to 0.25
- route_expert: int32 [3072, 8], P('expert'), may hold values from 0 to 31, all different within a row; in each aligned block of 96 rows (0 to 95, 96 to 191, ...) at most 32 rows name the same one
- cotangent: bfloat16 [3072, 4096], P('expert', 'dp'), may hold values from -6 to 6
- gate_quant: bfloat16 [32, 4096, 1024], P('expert', None, 'dp'), may hold values from -0.09375 to 0.09375
- up_quant: bfloat16 [32, 4096, 1024], P('expert', None, 'dp'), may hold values from -0.09375 to 0.09375
- gate_scale: float32 [32, 32, 8], P('expert', None, 'dp'), may hold values from 0.5 to 2
- up_scale: float32 [32, 32, 8], P('expert', None, 'dp'), may hold values from 0.5 to 2
- down_quant: bfloat16 [32, 1024, 4096], P('expert', None, 'dp'), may hold values from -0.1875 to 0.1875
- down_scale: float32 [32, 8, 32], P('expert', None, 'dp'), may hold values from 0.5 to 2
- first_moment: float32 [32, 1024, 4096], P('expert', None, 'dp'), may hold values from -6 to 6
- second_moment: float32 [32, 1024, 4096], P('expert', None, 'dp'), may hold values from 0.5 to 8
- old_expert: int32 [32], replicated, may hold values from 0 to 31, each once
- new_holder: int32 [32], replicated, may hold values from 0 to 31, each once
Outputs:
- mixed: bfloat16 [3072, 4096], P('expert', 'dp')
- new_down: bfloat16 [32, 1024, 4096], P('expert', None, 'dp')
- new_first: float32 [32, 1024, 4096], P('expert', None, 'dp')
- new_second: float32 [32, 1024, 4096], P('expert', None, 'dp')
The draws below stay inside these ranges and needn't reach their ends.
Inputs may be any that keep to these rules, and one draw needn't show every extreme that they name: `route_expert`: within each aligned block of 96 tokens (the tokens of one index of expert) no expert is named by more than 32 routes, a bound that some block reaches; a token names 8 different experts. `old_expert`: A permutation of the experts. `new_holder`: A permutation of the indices of expert.
All inputs are finite; a program needn't handle non-finite values.
Results may differ from the reference program's by a relative error of at most 0.0076.
Values may be sent and summed in bfloat16 or wider, within the bound.
A program may use at most 128 MiB of HBM per device.

```python
import math
import jax
import jax.numpy as jnp
import numpy as np
from jax import lax

D = 4096
TOPK = 8
H = 1024
QB = 128
T_DEV = 96
EXPERTS = 32
TOKENS = 3072
CAP = 32


def block_scale(rng, extent, split, smallest, top_value):
    gain = 1.0
    for dim, blocks in split:
        draws = jax.random.uniform(jax.random.fold_in(jax.random.fold_in(rng, 6), dim), (blocks,), jnp.float32, smallest / len(split), top_value / len(split))
        gain = gain * jnp.repeat(jnp.exp(draws), extent[dim] // blocks).reshape((-1,) + (1,) * (len(extent) - 1 - dim))
    return gain


def shared_out(own_key, own, number, rows, number_of, top, limit, skew):
    order = jax.random.permutation(own_key, number_of)
    crowded, ordinary = load_shares(number_of, rows * top, limit, skew, True), load_shares(number_of, rows * top, limit, skew, False)
    places = jnp.arange(number_of)

    def named(sizes, offset_by):
        used = int((sizes > 0).sum())
        fixed = max(1, used // 4)
        passed = fixed + (places - fixed + offset_by * (used - fixed)) % max(1, number_of - fixed)
        return jnp.zeros((number_of,), jnp.int32).at[order[jnp.where(places < fixed, places, passed)]].set(jnp.asarray(sizes, jnp.int32))

    sizes = jnp.where(number % 4 == 0, named(crowded, number // 4), named(ordinary, number - number // 4 - 1))
    mixed = jax.random.permutation(jax.random.fold_in(own, 3), number_of)
    giver, sink = mixed[0:number_of // 2 * 2:2], mixed[1:number_of // 2 * 2:2]
    room = jnp.minimum(sizes[giver] - 1, limit - sizes[sink]) // 2
    room = jnp.where((giver == order[0]) | (sink == order[0]) | (sizes[sink] == 0), 0, jnp.maximum(room, 0))
    passed = jax.random.randint(jax.random.fold_in(own, 4), (number_of // 2,), 0, 1 << 20) % (room + 1)
    sizes = sizes.at[giver].add(-passed).at[sink].add(passed)
    members = jnp.searchsorted(jnp.cumsum(sizes), jnp.arange(rows * top), side="right").astype(jnp.int32)
    table = members.reshape(top, rows).T
    table = table[jax.random.permutation(jax.random.fold_in(own, 1), rows)]
    offset_by = jax.random.randint(jax.random.fold_in(own, 2), (rows, 1), 0, top)
    return jnp.take_along_axis(table, (jnp.arange(top)[None, :] + offset_by) % top, axis=1)


def load_shares(number_of, total, bound, slope, full):
    loads = [(1 << 20) // math.isqrt(rank ** slope) + 1 for rank in range(1, number_of + 1)]
    largest = bound if full else min(bound, max(-(-total // number_of), total * loads[0] // sum(loads)))
    least = 1 if total - largest >= number_of - 1 else 0
    counts, rest = [largest] + [least] * (number_of - 1), total - largest - least * (number_of - 1)
    while rest > 0:
        free = [i for i in range(1, number_of) if counts[i] < largest] or [i for i in range(1, number_of) if counts[i] < bound]
        pool, budget = sum([loads[i] for i in free]), rest
        for i in free:
            addition = min(bound - counts[i], max(1, budget * loads[i] // pool), rest)
            counts[i] = counts[i] + addition
            rest = rest - addition
    return np.array(counts)


def centred(stream_key, extent, spread, most, pieces=(), held_as=jnp.bfloat16):
    level = block_scale(stream_key, extent, pieces, -0.22, 0.18) if pieces else 1.0
    entries = jax.random.normal(stream_key, extent, jnp.float32) * spread * level
    return jnp.minimum(jnp.maximum(entries, -most), most).astype(held_as)


def setup_inputs(seed: int = 0) -> dict:
    keys = jax.random.split(jax.random.key(seed), 15)
    tokens = centred(keys[0], (TOKENS, D), 1.0, 6.0, ((0, 32), (1, 8)))
    route_weight = jnp.clip(0.05 + 0.2 * jax.random.uniform(keys[1], (TOKENS, TOPK), jnp.float32) ** block_scale(keys[1], (TOKENS, TOPK), ((0, 32),), -0.2, 0.2), 0.05, 0.25)
    route_expert_keys = jax.random.split(jax.random.fold_in(keys[2], 1), TOKENS // T_DEV)
    route_expert_turns = jax.random.permutation(jax.random.fold_in(keys[2], 3), TOKENS // T_DEV)
    route_expert = jax.vmap(lambda own, number: shared_out(jax.random.fold_in(keys[2], 2), own, number, T_DEV, EXPERTS, TOPK, CAP, 1))(route_expert_keys, route_expert_turns).reshape((TOKENS, TOPK))
    cotangent = centred(keys[3], (TOKENS, D), 1.0, 6.0, ((0, 32), (1, 8)))
    gate_quant = centred(keys[4], (EXPERTS, D, H), D ** -0.5, 0.09375, ((0, 32), (2, 8)))
    up_quant = centred(keys[5], (EXPERTS, D, H), D ** -0.5, 0.09375, ((0, 32), (2, 8)))
    gate_scale = jnp.clip(jnp.exp(math.log(2.0) - 1.3862944 * jax.random.uniform(keys[6], (EXPERTS, D // QB, H // QB), jnp.float32) ** block_scale(keys[6], (EXPERTS, D // QB, H // QB), ((0, 32), (2, 8)), -0.2, 0.2)), 0.5, 2.0)
    up_scale = jnp.clip(jnp.exp(math.log(2.0) - 1.3862944 * jax.random.uniform(keys[7], (EXPERTS, D // QB, H // QB), jnp.float32) ** block_scale(keys[7], (EXPERTS, D // QB, H // QB), ((0, 32), (2, 8)), -0.2, 0.2)), 0.5, 2.0)
    down_quant = centred(keys[8], (EXPERTS, H, D), H ** -0.5, 0.1875, ((0, 32), (2, 8)))
    down_scale = jnp.clip(jnp.exp(math.log(2.0) - 1.3862944 * jax.random.uniform(keys[9], (EXPERTS, H // QB, D // QB), jnp.float32) ** block_scale(keys[9], (EXPERTS, H // QB, D // QB), ((0, 32), (2, 8)), -0.2, 0.2)), 0.5, 2.0)
    first_moment = centred(keys[10], (EXPERTS, H, D), 1.0, 6.0, ((0, 32), (2, 8)), jnp.float32)
    second_moment = jnp.clip(jnp.exp(math.log(8.0) - 2.7725887 * jax.random.uniform(keys[11], (EXPERTS, H, D), jnp.float32) ** block_scale(keys[11], (EXPERTS, H, D), ((0, 32), (2, 8)), -0.2, 0.2)), 0.5, 8.0)
    old_expert = jax.random.permutation(keys[12], EXPERTS).astype(jnp.int32)
    new_holder = jax.random.permutation(keys[13], EXPERTS).astype(jnp.int32)
    return {"tokens": tokens, "route_weight": route_weight, "route_expert": route_expert, "cotangent": cotangent, "gate_quant": gate_quant, "up_quant": up_quant, "gate_scale": gate_scale, "up_scale": up_scale, "down_quant": down_quant, "down_scale": down_scale, "first_moment": first_moment, "second_moment": second_moment, "old_expert": old_expert, "new_holder": new_holder}


beta_first = 0.9
beta_second = 0.95
adam_eps = 1e-08
learn_rate = 0.003
decay_rate = 0.1
step_count = 20

def dequantize(quant, scale):
    tiled = jnp.repeat(jnp.repeat(scale, QB, axis=0), QB, axis=1)
    return quant.astype(jnp.float32) * tiled

def adam_step(master, grad, first, second):
    first_new = beta_first * first + (1.0 - beta_first) * grad
    second_new = beta_second * second + (1.0 - beta_second) * grad * grad
    fix_first = 1.0 - beta_first ** step_count
    fix_second = 1.0 - beta_second ** step_count
    update = first_new / fix_first / (jnp.sqrt(second_new / fix_second) + adam_eps)
    fresh = (master - learn_rate * (update + decay_rate * master)).astype(jnp.bfloat16)
    return (fresh, first_new, second_new)

def reference(tokens, route_weight, route_expert, cotangent, gate_quant, up_quant, gate_scale, up_scale, down_quant, down_scale, first_moment, second_moment, old_expert, new_holder):
    route_count = TOKENS * TOPK
    rows_most = TOKENS // T_DEV * CAP
    flat_expert = route_expert.reshape(-1)
    flat_weight = route_weight.reshape(-1)
    route_ids = jnp.arange(route_count, dtype=jnp.int32)

    def per_expert(total, index):
        expert_id = old_expert[index]
        hit_mask = (flat_expert == expert_id).astype(jnp.int32)
        order_pos = jnp.cumsum(hit_mask) - 1
        target_pos = jnp.where(hit_mask > 0, order_pos, rows_most).astype(jnp.int32)
        slot_route = jnp.full((rows_most,), route_count, jnp.int32).at[target_pos].set(route_ids, mode='drop')
        live_rows = slot_route < route_count
        safe_route = jnp.minimum(slot_route, route_count - 1)
        token_ids = safe_route // TOPK
        rows_in = jnp.where(live_rows[:, None], tokens[token_ids], jnp.zeros((), jnp.bfloat16))
        gate_w = dequantize(gate_quant[index], gate_scale[index]).astype(jnp.bfloat16)
        up_w = dequantize(up_quant[index], up_scale[index]).astype(jnp.bfloat16)
        master = dequantize(down_quant[index], down_scale[index])
        down_w = master.astype(jnp.bfloat16)
        gate_val = jnp.dot(rows_in, gate_w, preferred_element_type=jnp.float32)
        up_val = jnp.dot(rows_in, up_w, preferred_element_type=jnp.float32)
        hidden = (jax.nn.silu(gate_val) * up_val).astype(jnp.bfloat16)
        out_rows = jnp.dot(hidden, down_w, preferred_element_type=jnp.float32).astype(jnp.bfloat16)
        weight_rows = jnp.where(live_rows, flat_weight[safe_route], jnp.float32(0.0))
        total = total.at[token_ids].add(weight_rows[:, None] * out_rows.astype(jnp.float32))
        back_rows = (weight_rows[:, None] * cotangent[token_ids].astype(jnp.float32)).astype(jnp.bfloat16)
        grad = lax.dot_general(hidden, back_rows, (((0,), (0,)), ((), ())), preferred_element_type=jnp.float32)
        fresh, first_new, second_new = adam_step(master, grad, first_moment[index], second_moment[index])
        return (total, (fresh, first_new, second_new))
    start = jnp.zeros((TOKENS, D), jnp.float32)
    total, stacked = lax.scan(per_expert, start, jnp.arange(EXPERTS, dtype=jnp.int32))
    labels = jnp.arange(EXPERTS, dtype=jnp.int32)
    takes = (new_holder[:, None] == labels[None, :]).astype(jnp.int32)
    giver = lax.optimization_barrier(jnp.sum(takes * labels[:, None], axis=0)).astype(jnp.int32)
    fresh_all, first_all, second_all = stacked
    return (total.astype(jnp.bfloat16), fresh_all[giver], first_all[giver], second_all[giver])
```

```python
import jax
import jax.numpy as jnp
from jax import lax
from jax.experimental import pallas as pl
from jax.experimental.pallas import tpu as pltpu
from jax.sharding import PartitionSpec as P

QB = 128
BF = jnp.bfloat16
F32 = jnp.float32

beta_first = 0.9
beta_second = 0.95
adam_eps = 1e-08
learn_rate = 0.003
decay_rate = 0.1
step_count = 20
fix_first = 1.0 - beta_first**step_count
fix_second = 1.0 - beta_second**step_count

VMEM_LIMIT = 48 * 1024 * 1024


def split_bits(value):
    high = lax.reduce_precision(value, 8, 7)
    rest = value - high
    middle = lax.reduce_precision(rest, 8, 7)
    low = rest - middle
    return high.astype(BF), middle.astype(BF), low.astype(BF)


def ranks(mask):
    count = mask.shape[-1]
    i = jnp.arange(count)
    earlier = (i[:, None] < i[None, :]).astype(BF)
    position = jnp.dot(mask.astype(BF), earlier, preferred_element_type=F32)
    return jnp.where(mask > 0, position, -1.0)


def compact_kernel(rank_ref, table_ref, out_ref):
    blocks, rows, _ = table_ref.shape
    slots = out_ref.shape[0] // blocks
    for s in range(blocks):
        place = lax.broadcasted_iota(jnp.int32, (slots, rows), 0).astype(F32)
        pick = (rank_ref[s : s + 1, :] == place).astype(BF)
        picked = jnp.dot(pick, table_ref[s], preferred_element_type=F32)
        out_ref[s * slots : (s + 1) * slots, :] = picked.astype(BF)


def compact(rank, table, slots, width):
    blocks, rows, _ = table.shape
    return pl.pallas_call(
        compact_kernel,
        grid=(1,),
        in_specs=[
            pl.BlockSpec((blocks, rows), lambda i: (0, 0)),
            pl.BlockSpec((blocks, rows, width), lambda i: (0, 0, 0)),
        ],
        out_specs=pl.BlockSpec((blocks * slots, width), lambda i: (0, 0)),
        out_shape=jax.ShapeDtypeStruct((blocks * slots, width), BF),
        compiler_params=pltpu.CompilerParams(vmem_limit_bytes=VMEM_LIMIT),
        cost_estimate=pl.CostEstimate(
            flops=2 * blocks * slots * rows * width, bytes_accessed=4 << 20, transcendentals=0
        ),
        name="compact",
    )(rank, table)


def back_kernel(rank_ref, weight_ref, table_ref, out_ref):
    blocks, rows, _ = table_ref.shape
    slots = out_ref.shape[0] // blocks
    for s in range(blocks):
        place = lax.broadcasted_iota(jnp.int32, (slots, rows), 0).astype(F32)
        hit = rank_ref[s : s + 1, :] == place
        weight = jnp.sum(jnp.where(hit, weight_ref[s : s + 1, :], 0.0), axis=1, keepdims=True)
        picked = jnp.dot(hit.astype(BF), table_ref[s], preferred_element_type=F32)
        out_ref[s * slots : (s + 1) * slots, :] = (weight * picked).astype(BF)


def weighted_compact(rank, weight, table, slots, width):
    blocks, rows, _ = table.shape
    return pl.pallas_call(
        back_kernel,
        grid=(1,),
        in_specs=[
            pl.BlockSpec((blocks, rows), lambda i: (0, 0)),
            pl.BlockSpec((blocks, rows), lambda i: (0, 0)),
            pl.BlockSpec((blocks, rows, width), lambda i: (0, 0, 0)),
        ],
        out_specs=pl.BlockSpec((blocks * slots, width), lambda i: (0, 0)),
        out_shape=jax.ShapeDtypeStruct((blocks * slots, width), BF),
        compiler_params=pltpu.CompilerParams(vmem_limit_bytes=VMEM_LIMIT),
        cost_estimate=pl.CostEstimate(
            flops=2 * blocks * slots * rows * width, bytes_accessed=4 << 20, transcendentals=0
        ),
        name="back_rows",
    )(rank, weight, table)


def gate_up_kernel(gs_ref, us_ref, x_ref, gq_ref, uq_ref, out_ref, acc_ref):
    k = pl.program_id(0)
    depth, hidden = gq_ref.shape
    per = depth // QB

    @pl.when(k == 0)
    def _():
        acc_ref[...] = jnp.zeros_like(acc_ref)

    gates, ups = [], []
    for j in range(per):
        rows = slice(j * QB, (j + 1) * QB)
        gates.append((gq_ref[rows, :].astype(F32) * gs_ref[k * per + j]).astype(BF))
        ups.append((uq_ref[rows, :].astype(F32) * us_ref[k * per + j]).astype(BF))
    weights = jnp.concatenate(
        [jnp.concatenate(gates, axis=0), jnp.concatenate(ups, axis=0)], axis=1
    )
    acc_ref[...] += jnp.dot(x_ref[0], weights, preferred_element_type=F32)

    @pl.when(k == pl.num_programs(0) - 1)
    def _():
        gate = acc_ref[:, :hidden]
        up = acc_ref[:, hidden:]
        out_ref[...] = (gate / (1.0 + jnp.exp(-gate)) * up).astype(BF)


def gate_up(rows_in, gate_quant, up_quant, gate_scale, up_scale):
    parts, rows, depth = rows_in.shape
    hidden = gate_quant.shape[1]
    return pl.pallas_call(
        gate_up_kernel,
        grid=(parts,),
        in_specs=[
            pl.BlockSpec(memory_space=pltpu.SMEM),
            pl.BlockSpec(memory_space=pltpu.SMEM),
            pl.BlockSpec((1, rows, depth), lambda k: (k, 0, 0)),
            pl.BlockSpec((depth, hidden), lambda k: (k, 0)),
            pl.BlockSpec((depth, hidden), lambda k: (k, 0)),
        ],
        out_specs=pl.BlockSpec((rows, hidden), lambda k: (0, 0)),
        out_shape=jax.ShapeDtypeStruct((rows, hidden), BF),
        scratch_shapes=[pltpu.VMEM((rows, 2 * hidden), F32)],
        compiler_params=pltpu.CompilerParams(vmem_limit_bytes=VMEM_LIMIT),
        cost_estimate=pl.CostEstimate(
            flops=4 * parts * rows * depth * hidden, bytes_accessed=11 << 20, transcendentals=0
        ),
        name="gate_up",
    )(gate_scale, up_scale, rows_in, gate_quant, up_quant)


def master_rows(quant, scale_ref, tile_row):
    parts = []
    for c in range(quant.shape[1] // QB):
        parts.append(quant[:, c * QB : (c + 1) * QB].astype(F32) * scale_ref[tile_row, c])
    return jnp.concatenate(parts, axis=1)


def down_kernel(scale_ref, hidden_ref, quant_ref, out_ref, acc_ref):
    k = pl.program_id(0)
    pieces, _, piece_rows, width = quant_ref.shape

    @pl.when(k == 0)
    def _():
        acc_ref[...] = jnp.zeros_like(acc_ref)

    quant = quant_ref[...].reshape(pieces * piece_rows, width)
    down_w = master_rows(quant, scale_ref, k).astype(BF)
    acc_ref[...] += jnp.dot(hidden_ref[0], down_w, preferred_element_type=F32)

    @pl.when(k == pl.num_programs(0) - 1)
    def _():
        out_ref[...] = acc_ref[...].astype(BF)


def down(hidden, state, scale):
    parts, rows, part_hidden = hidden.shape
    number, _, piece_rows, width = state.shape
    pieces = number // parts
    return pl.pallas_call(
        down_kernel,
        grid=(parts,),
        in_specs=[
            pl.BlockSpec(memory_space=pltpu.SMEM),
            pl.BlockSpec((1, rows, part_hidden), lambda k: (k, 0, 0)),
            pl.BlockSpec((pieces, 1, piece_rows, width), lambda k: (k, 2, 0, 0)),
        ],
        out_specs=pl.BlockSpec((rows, width), lambda k: (0, 0)),
        out_shape=jax.ShapeDtypeStruct((rows, width), BF),
        scratch_shapes=[pltpu.VMEM((rows, width), F32)],
        compiler_params=pltpu.CompilerParams(vmem_limit_bytes=VMEM_LIMIT),
        cost_estimate=pl.CostEstimate(
            flops=2 * parts * rows * part_hidden * width, bytes_accessed=4 << 20, transcendentals=0
        ),
        name="down",
    )(scale, hidden, state)


def adam_kernel(scale_ref, hidden_ref, back_ref, state_ref, down_ref, first_ref, second_ref):
    k = pl.program_id(0)
    pieces, _, piece_rows, width = state_ref.shape
    rows = pieces * piece_rows
    grad = lax.dot_general(
        hidden_ref[0], back_ref[...], (((0,), (0,)), ((), ())), preferred_element_type=F32
    )
    first = state_ref[:, 0].reshape(rows, width).astype(F32)
    second = state_ref[:, 1].reshape(rows, width).astype(F32)
    master = master_rows(state_ref[:, 2].reshape(rows, width), scale_ref, k)
    first_new = beta_first * first + (1.0 - beta_first) * grad
    second_new = beta_second * second + (1.0 - beta_second) * grad * grad
    update = first_new / fix_first / (jnp.sqrt(second_new / fix_second) + adam_eps)
    down_ref[0] = (master - learn_rate * (update + decay_rate * master)).astype(BF)
    first_ref[0] = first_new
    second_ref[0] = second_new


def grad_adam(hidden, back, state, scale):
    parts, rows, part_hidden = hidden.shape
    number, kinds, piece_rows, width = state.shape
    pieces = number // parts
    total = number * piece_rows
    block = pl.BlockSpec((1, part_hidden, width), lambda k: (0, k, 0))
    return pl.pallas_call(
        adam_kernel,
        grid=(parts,),
        in_specs=[
            pl.BlockSpec(memory_space=pltpu.SMEM),
            pl.BlockSpec((1, rows, part_hidden), lambda k: (k, 0, 0)),
            pl.BlockSpec((rows, width), lambda k: (0, 0)),
            pl.BlockSpec((pieces, kinds, piece_rows, width), lambda k: (k, 0, 0, 0)),
        ],
        out_specs=[block, block, block],
        out_shape=[
            jax.ShapeDtypeStruct((1, total, width), BF),
            jax.ShapeDtypeStruct((1, total, width), F32),
            jax.ShapeDtypeStruct((1, total, width), F32),
        ],
        compiler_params=pltpu.CompilerParams(vmem_limit_bytes=VMEM_LIMIT),
        cost_estimate=pl.CostEstimate(
            flops=2 * parts * rows * part_hidden * width, bytes_accessed=11 << 20, transcendentals=0
        ),
        name="grad_adam",
    )(scale, hidden, back, state)


def mix_kernel(slots, rank_ref, weight_ref, rows_ref, out_ref):
    number = rank_ref.shape[1]
    total = number * slots
    holder = lax.broadcasted_iota(jnp.int32, (number, total), 0)
    column = lax.broadcasted_iota(jnp.int32, (number, total), 1)
    spread = (column // slots == holder).astype(BF)
    place = lax.broadcasted_iota(jnp.int32, (rank_ref.shape[0], total), 1) % slots
    rank = jnp.dot(rank_ref[...].astype(BF), spread, preferred_element_type=F32)
    hit = rank == place.astype(F32)
    rest = weight_ref[...]
    acc = jnp.zeros(out_ref.shape, F32)
    for _ in range(3):
        piece = rest.astype(BF)
        rest = rest - piece.astype(F32)
        wide = jnp.dot(piece, spread, preferred_element_type=F32)
        chosen = jnp.where(hit, wide, 0.0).astype(BF)
        acc += jnp.dot(chosen, rows_ref[...], preferred_element_type=F32)
    out_ref[...] = acc.astype(BF)


def mix(rank, weight, rows, slots):
    tokens = rank.shape[0]
    width = rows.shape[1]

    def kernel(*refs):
        mix_kernel(slots, *refs)

    return pl.pallas_call(
        kernel,
        out_shape=jax.ShapeDtypeStruct((tokens, width), BF),
        compiler_params=pltpu.CompilerParams(vmem_limit_bytes=VMEM_LIMIT),
        cost_estimate=pl.CostEstimate(
            flops=6 * tokens * rows.shape[0] * width, bytes_accessed=1 << 20, transcendentals=0
        ),
        name="mix",
    )(rank, weight, rows)


def reorder_kernel(index_ref, in_ref, out_ref):
    for j in range(in_ref.shape[0]):
        out_ref[j] = in_ref[index_ref[j]]


def reorder(pieces, index):
    return pl.pallas_call(
        reorder_kernel,
        in_specs=[
            pl.BlockSpec(memory_space=pltpu.SMEM),
            pl.BlockSpec(memory_space=pltpu.VMEM),
        ],
        out_shape=jax.ShapeDtypeStruct(pieces.shape, pieces.dtype),
        compiler_params=pltpu.CompilerParams(vmem_limit_bytes=VMEM_LIMIT),
        cost_estimate=pl.CostEstimate(
            flops=0, bytes_accessed=2 * pieces.size * pieces.dtype.itemsize, transcendentals=0
        ),
        name="reorder",
    )(index, pieces)


def swap(pieces):
    return lax.all_to_all(pieces, "expert", split_axis=0, concat_axis=0, tiled=True)


def per_device(
    tokens,
    route_weight,
    route_expert,
    cotangent,
    gate_quant,
    up_quant,
    gate_scale,
    up_scale,
    down_quant,
    down_scale,
    first_moment,
    second_moment,
    old_expert,
    new_holder,
):
    number = lax.axis_size("expert")
    me = lax.axis_index("expert")
    tok_rows, top_count = route_expert.shape
    width = cotangent.shape[1]
    slots = min(tok_rows, tok_rows * top_count // number * 4 // 3)
    hidden_total = down_quant.shape[1]
    labels = jnp.arange(number, dtype=jnp.int32)
    giver = jnp.sum((new_holder[:, None] == labels[None, :]) * labels[:, None], axis=0)
    held = jnp.sum((new_holder[:, None] == labels[None, :]) * old_expert[:, None], axis=0)
    mine = labels == me
    expert_before = jnp.sum(jnp.where(mine, old_expert, 0))
    expert_after = jnp.sum(jnp.where(mine, held, 0))
    my_giver = jnp.sum(jnp.where(mine, giver, 0))

    scale_parts = jnp.concatenate(split_bits(down_scale[0]), axis=1)
    scale_rows, scale_cols = scale_parts.shape
    extra = jnp.concatenate(
        [
            route_expert.astype(BF),
            *split_bits(route_weight),
            jnp.pad(scale_parts, ((0, tok_rows - scale_rows), (0, QB - 4 * top_count - scale_cols))),
        ],
        axis=1,
    )
    gathered = lax.all_gather(jnp.concatenate([tokens, extra], axis=1), "expert", axis=0)
    table = gathered[:, :, width:].astype(F32)
    routes = table[:, :, :top_count]
    weights = (
        table[:, :, top_count : 2 * top_count]
        + table[:, :, 2 * top_count : 3 * top_count]
        + table[:, :, 3 * top_count : 4 * top_count]
    )
    third = scale_cols // 3
    scales = table[:, :scale_rows, 4 * top_count : 4 * top_count + scale_cols]
    scales = scales[:, :, :third] + scales[:, :, third : 2 * third] + scales[:, :, 2 * third :]
    new_scale = jnp.sum(jnp.where((labels == my_giver)[:, None, None], scales, 0.0), axis=0)
    rank_before = ranks(jnp.sum(jnp.where(routes == expert_before.astype(F32), 1.0, 0.0), axis=2))
    hit_after = routes == expert_after.astype(F32)
    rank_after = ranks(jnp.sum(jnp.where(hit_after, 1.0, 0.0), axis=2))
    weight_after = jnp.sum(jnp.where(hit_after, weights, 0.0), axis=2)

    piece_rows = hidden_total // number
    state = jnp.stack(
        [
            first_moment[0].astype(BF).reshape(number, piece_rows, width),
            second_moment[0].astype(BF).reshape(number, piece_rows, width),
            down_quant[0].reshape(number, piece_rows, width),
        ],
        axis=1,
    )
    spread = swap(state)

    cot_all = lax.all_gather(cotangent, "expert", axis=0)

    sent = compact(rank_before, gathered, slots, width)
    rows_in = lax.all_gather(sent, "dp", axis=0)
    hidden_part = gate_up(
        rows_in, gate_quant[0], up_quant[0], gate_scale.reshape(-1), up_scale.reshape(-1)
    )
    hidden_part, spread = lax.optimization_barrier((hidden_part, spread))
    state = swap(reorder(spread, giver))
    hidden_part = hidden_part.reshape(number, slots, -1)
    hidden_part = swap(reorder(swap(hidden_part), giver)).reshape(number * slots, -1)
    hidden = lax.all_gather(hidden_part, "dp", axis=0)

    out_rows = down(hidden, state, new_scale)
    returned = swap(out_rows.reshape(number, slots, width)).reshape(-1, width)
    back = weighted_compact(rank_after, weight_after, cot_all, slots, width)
    fresh, first_new, second_new = grad_adam(hidden, back, state, new_scale)

    chosen = route_expert[:, :, None] == held[None, None, :]
    own_rank = ranks(jnp.sum(chosen.astype(F32), axis=1).T).T
    own_weight = jnp.sum(jnp.where(chosen, route_weight[:, :, None], 0.0), axis=1)
    mixed = mix(own_rank, own_weight, returned, slots)
    return (mixed, fresh, first_new, second_new)


def solution(mesh):
    in_specs = (
        P("expert", "dp"),
        P("expert", None),
        P("expert", None),
        P("expert", "dp"),
        P("expert", None, "dp"),
        P("expert", None, "dp"),
        P("expert", None, "dp"),
        P("expert", None, "dp"),
        P("expert", None, "dp"),
        P("expert", None, "dp"),
        P("expert", None, "dp"),
        P("expert", None, "dp"),
        P(),
        P(),
    )
    out_specs = (
        P("expert", "dp"),
        P("expert", None, "dp"),
        P("expert", None, "dp"),
        P("expert", None, "dp"),
    )
    return jax.shard_map(
        per_device, mesh=mesh, in_specs=in_specs, out_specs=out_specs, check_vma=False
    )
```

```python
import jax
import jax.numpy as jnp
from jax import lax
from jax.experimental import pallas as pl
from jax.experimental.pallas import tpu as pltpu
from jax.sharding import PartitionSpec as P

QB = 128
BF = jnp.bfloat16
F32 = jnp.float32
MESH = pl.DeviceIdType.MESH

beta_first = 0.9
beta_second = 0.95
adam_eps = 1e-08
learn_rate = 0.003
decay_rate = 0.1
step_count = 20
fix_first = 1.0 - beta_first**step_count
fix_second = 1.0 - beta_second**step_count

VMEM_LIMIT = 58 * 1024 * 1024

T, SC, D1, F1, S1, B, D2, F2, S2, H1, H2, O, Y1, Y2, W = range(15)
KINDS = 15


def transposed_dot(a, b):
    return lax.dot_general(a, b, (((0,), (0,)), ((), ())), preferred_element_type=F32)


def step_kernel(
    giver_ref,
    my_giver_ref,
    gate_scale_ref,
    up_scale_ref,
    before_ref,
    after_ref,
    route_ref,
    weight_ref,
    tok_ref,
    cot_ref,
    scale_ref,
    gate_hbm,
    up_hbm,
    down_hbm,
    first_hbm,
    second_hbm,
    mixed_ref,
    fresh_ref,
    first_ref,
    second_ref,
    tok_send,
    tok_recv,
    scale_all,
    down_mid,
    first_send,
    first_mid,
    second_send,
    second_mid,
    back_send,
    back_recv,
    down_out,
    down_new,
    first_out,
    first_new,
    second_out,
    second_new,
    hid_send,
    hid_mid,
    hid_out,
    hid_new,
    out_send,
    out_recv,
    rows_all,
    weights_all,
    gate_v,
    up_v,
    hidden_all,
    grad_ref,
    pick_ref,
    send_sem,
    recv_sem,
    local_sem,
    load_sem,
):
    number = lax.axis_size("expert")
    parts = lax.axis_size("dp")
    cores = weights_all.shape[0]
    e = lax.axis_index("expert")
    d = lax.axis_index("dp")
    core = lax.rem(d, cores)
    tokens, width = tok_ref.shape
    slots = tok_send.shape[1]
    total = number * slots
    half = number // cores
    half_rows = half * slots
    hidden_part = gate_v.shape[1]

    def remote(src, dst, kind, target):
        return pltpu.make_async_remote_copy(
            src_ref=src,
            dst_ref=dst,
            send_sem=send_sem.at[kind],
            recv_sem=recv_sem.at[kind],
            device_id=target,
            device_id_type=MESH,
        )

    loads = [
        pltpu.make_async_copy(src, dst, load_sem.at[i])
        for i, (src, dst) in enumerate(
            [
                (gate_hbm, gate_v),
                (up_hbm, up_v),
                (first_hbm, first_ref),
                (second_hbm, second_ref),
            ]
        )
    ]
    for load in loads:
        load.start()

    barrier = pltpu.get_barrier_semaphore()

    def greet_expert(k, carry):
        pl.semaphore_signal(
            barrier, inc=1, device_id=(lax.rem(e + k, number), d), device_id_type=MESH
        )
        return carry

    def greet_dp(k, carry):
        pl.semaphore_signal(
            barrier, inc=1, device_id=(e, lax.rem(d + k, parts)), device_id_type=MESH
        )
        return carry

    lax.fori_loop(1, number, greet_expert, 0)
    lax.fori_loop(1, parts, greet_dp, 0)

    i = lax.broadcasted_iota(jnp.int32, (tokens, tokens), 0)
    j = lax.broadcasted_iota(jnp.int32, (tokens, tokens), 1)
    earlier = (j < i).astype(BF)
    holder = lax.broadcasted_iota(jnp.int32, (number, total), 0)
    column = lax.broadcasted_iota(jnp.int32, (number, total), 1)
    spread = jnp.logical_and(column >= holder * slots, column < (holder + 1) * slots).astype(BF)
    place = lax.rem(lax.broadcasted_iota(jnp.int32, (tokens, total), 1), slots).astype(F32)

    def slot_hits(hit):
        rank = jnp.dot(earlier, hit.astype(BF), preferred_element_type=F32)
        rank = jnp.where(hit > 0.0, rank, -1.0)
        return jnp.dot(rank.astype(BF), spread, preferred_element_type=F32) == place

    routes = route_ref[...]
    hit_before = jnp.zeros((tokens, number), F32)
    hit_after = jnp.zeros((tokens, number), F32)
    weight_after = jnp.zeros((tokens, number), F32)
    for k in range(routes.shape[1]):
        named = routes[:, k : k + 1]
        hit_before += (named == before_ref[...]).astype(F32)
        match = named == after_ref[...]
        hit_after += match.astype(F32)
        weight_after += jnp.where(match, weight_ref[:, k : k + 1], 0.0)

    pick = slot_hits(hit_before).astype(BF)
    tok_send[...] = transposed_dot(pick, tok_ref[...]).astype(BF).reshape(tok_send.shape)

    pl.semaphore_wait(barrier, number - 1 + parts - 1)

    def send_all(src, dst, kind, same=False):
        def body(k, carry):
            t = lax.rem(e + k, number)
            remote(src if same else src.at[t], dst.at[e], kind, (t, d)).start()
            return carry

        lax.fori_loop(1, number, body, 0)
        pltpu.make_async_copy(src if same else src.at[e], dst.at[e], local_sem.at[kind]).start()

    def wait_all(src, dst, kind, same=False):
        rest = dst.at[pl.ds(0, number - 1)]
        remote(rest, rest, kind, (lax.rem(e + 1, number), d)).wait_recv()
        pltpu.make_async_copy(src if same else src.at[e], dst.at[e], local_sem.at[kind]).wait()

    def sent_all(dst, kind):
        rest = dst.at[pl.ds(0, number - 1)]
        remote(rest, rest, kind, (lax.rem(e + 1, number), d)).wait_send()

    def reorder(src, dst):
        def body(k, carry):
            dst[k] = src[giver_ref[k]]
            return carry

        lax.fori_loop(0, number, body, 0)

    send_all(tok_send, tok_recv, T)
    send_all(scale_ref, scale_all, SC, same=True)

    loads[0].wait()
    loads[1].wait()

    def dequantize(r, carry):
        rows = pl.ds(pl.multiple_of(r * QB, QB), QB)
        gate = (gate_v[rows, :].astype(F32) * gate_scale_ref[r]).astype(BF)
        up = (up_v[rows, :].astype(F32) * up_scale_ref[r]).astype(BF)
        weights_all[core, rows, :] = jnp.concatenate([gate, up], axis=1)
        return carry

    lax.fori_loop(0, gate_v.shape[0] // QB, dequantize, 0)
    sibling = (e, d + 1 - 2 * core)
    weights_copy = remote(weights_all.at[core], weights_all.at[core], W, sibling)
    weights_copy.start()

    hit_slots = slot_hits(hit_after)
    rest = weight_after
    for p in range(3):
        piece = rest.astype(BF)
        rest = rest - piece.astype(F32)
        wide = jnp.dot(piece, spread, preferred_element_type=F32)
        pick_ref[p] = jnp.where(hit_slots, wide, 0.0).astype(BF)

    loads[2].wait()
    first_send[...] = first_ref[...].astype(BF).reshape(first_send.shape)
    loads[3].wait()
    second_send[...] = second_ref[...].astype(BF).reshape(second_send.shape)

    sent_all(tok_recv, T)
    send_all(down_hbm, down_mid, D1)
    back = transposed_dot(pick_ref[0], cot_ref[...])
    back += transposed_dot(pick_ref[1], cot_ref[...])
    back += transposed_dot(pick_ref[2], cot_ref[...])
    back_send[...] = back.astype(BF).reshape(back_send.shape)

    wait_all(tok_send, tok_recv, T)

    def send_rows(k, carry):
        t = lax.rem(d + k, parts)
        src = tok_recv.at[pl.ds(lax.rem(t, cores) * half, half)]
        remote(src, rows_all.at[d], Y1, (e, t)).start()
        return carry

    lax.fori_loop(1, parts, send_rows, 0)
    own_rows = pltpu.make_async_copy(
        tok_recv.at[pl.ds(core * half, half)], rows_all.at[d], local_sem.at[Y1]
    )
    own_rows.start()
    send_all(first_send, first_mid, F1)
    send_all(second_send, second_mid, S1)
    send_all(back_send, back_recv, B)

    wait_all(down_hbm, down_mid, D1)
    reorder(down_mid, down_out)
    send_all(down_out, down_new, D2)

    own_rows.wait()
    weights_copy.wait()
    others = rows_all.at[pl.ds(0, parts - 1)]
    remote(others, others, Y1, sibling).wait()
    for c in range(cores):
        value = jnp.zeros((half_rows, 2 * hidden_part), F32)
        for k in range(parts):
            value += jnp.dot(
                rows_all[k].reshape(half_rows, width),
                weights_all[c, k * width : (k + 1) * width, :],
                preferred_element_type=F32,
            )
        gate = value[:, :hidden_part]
        up = value[:, hidden_part:]
        act = (gate / (1.0 + jnp.exp(-gate)) * up).astype(BF)
        hid_send[:, :, c * hidden_part : (c + 1) * hidden_part] = act.reshape(
            number, half_rows // number, hidden_part
        )
    send_all(hid_send, hid_mid, H1)

    wait_all(first_send, first_mid, F1)
    reorder(first_mid, first_out)
    send_all(first_out, first_new, F2)

    wait_all(hid_send, hid_mid, H1)
    reorder(hid_mid, hid_out)
    send_all(hid_out, hid_new, H2)

    wait_all(second_send, second_mid, S1)
    reorder(second_mid, second_out)
    send_all(second_out, second_new, S2)

    wait_all(hid_out, hid_new, H2)

    def send_hidden(k, carry):
        remote(hid_new, hidden_all.at[d], Y2, (e, lax.rem(d + k, parts))).start()
        return carry

    lax.fori_loop(1, parts, send_hidden, 0)
    own_hidden = pltpu.make_async_copy(hid_new, hidden_all.at[d], local_sem.at[Y2])
    own_hidden.start()

    wait_all(scale_ref, scale_all, SC, same=True)
    wait_all(down_out, down_new, D2)
    scale = scale_all[my_giver_ref[0]]
    scale_wide = jnp.concatenate(
        [jnp.broadcast_to(scale[:, c : c + 1], (scale.shape[0], QB)) for c in range(width // QB)],
        axis=1,
    )
    pieces = QB // down_new.shape[1]

    def master_rows(r):
        quant = down_new[r * pieces : (r + 1) * pieces].reshape(QB, width)
        return quant.astype(F32) * scale_wide[r : r + 1, :]

    own_hidden.wait()
    others = hidden_all.at[pl.ds(0, parts - 1)]
    remote(others, others, Y2, sibling).wait()
    pair = cores * hidden_part
    for c in range(cores):
        value = jnp.zeros((half_rows, width), F32)
        for y in range(parts // cores):
            down_w = jnp.concatenate(
                [master_rows(y * pair // QB + r).astype(BF) for r in range(pair // QB)], axis=0
            )
            value += jnp.dot(
                hidden_all[y * cores + c].reshape(half_rows, pair),
                down_w,
                preferred_element_type=F32,
            )
        out_send[c * half : (c + 1) * half] = value.astype(BF).reshape(half, slots, width)
    send_all(out_send, out_recv, O)

    wait_all(back_send, back_recv, B)
    for y in range(parts // cores):
        value = jnp.zeros((pair, width), F32)
        for c in range(cores):
            value += transposed_dot(
                hidden_all[y * cores + c].reshape(half_rows, pair),
                back_recv[c * half : (c + 1) * half].reshape(half_rows, width),
            )
        grad_ref[y * pair : (y + 1) * pair, :] = value

    wait_all(first_out, first_new, F2)
    wait_all(second_out, second_new, S2)
    for r in range(grad_ref.shape[0] // QB):
        rows = slice(r * QB, (r + 1) * QB)
        block = slice(r * pieces, (r + 1) * pieces)
        grad = grad_ref[rows, :]
        master = master_rows(r)
        first = first_new[block].reshape(QB, width).astype(F32)
        second = second_new[block].reshape(QB, width).astype(F32)
        first = beta_first * first + (1.0 - beta_first) * grad
        second = beta_second * second + (1.0 - beta_second) * grad * grad
        update = first / fix_first / (jnp.sqrt(second / fix_second) + adam_eps)
        fresh_ref[rows, :] = (master - learn_rate * (update + decay_rate * master)).astype(BF)
        first_ref[rows, :] = first
        second_ref[rows, :] = second

    wait_all(out_send, out_recv, O)
    returned = out_recv[...].reshape(total, width)
    value = jnp.dot(pick_ref[0], returned, preferred_element_type=F32)
    value += jnp.dot(pick_ref[1], returned, preferred_element_type=F32)
    value += jnp.dot(pick_ref[2], returned, preferred_element_type=F32)
    mixed_ref[...] = value.astype(BF)

    for dst, kind in (
        (scale_all, SC),
        (down_mid, D1),
        (first_mid, F1),
        (second_mid, S1),
        (back_recv, B),
        (down_new, D2),
        (first_new, F2),
        (second_new, S2),
        (hid_mid, H1),
        (hid_new, H2),
        (out_recv, O),
    ):
        sent_all(dst, kind)


def per_device(
    tokens,
    route_weight,
    route_expert,
    cotangent,
    gate_quant,
    up_quant,
    gate_scale,
    up_scale,
    down_quant,
    down_scale,
    first_moment,
    second_moment,
    old_expert,
    new_holder,
):
    number = lax.axis_size("expert")
    parts = lax.axis_size("dp")
    cores = 2
    me = lax.axis_index("expert")
    tok_rows, top_count = route_expert.shape
    width = cotangent.shape[1]
    slots = min(tok_rows, tok_rows * top_count // number * 4 // 3)
    model_width, hidden_part = gate_quant.shape[1:]
    hidden_total = down_quant.shape[1]
    piece_rows = hidden_total // number
    labels = jnp.arange(number, dtype=jnp.int32)
    takes = new_holder[:, None] == labels[None, :]
    giver = jnp.sum(takes * labels[:, None], axis=0)
    held = jnp.sum(takes * old_expert[:, None], axis=0)
    my_giver = jnp.sum(jnp.where(new_holder == me, labels, 0)).reshape(1)
    scale = jnp.pad(down_scale[0], ((0, 0), (0, QB - down_scale.shape[2])))

    smem = pl.BlockSpec(memory_space=pltpu.SMEM)
    vmem = pl.BlockSpec(memory_space=pltpu.VMEM)
    hbm = pl.BlockSpec(memory_space=pl.ANY)
    state = pltpu.VMEM((number, piece_rows, width), BF)
    rows = pltpu.VMEM((number, slots, width), BF)
    half_rows = number * slots // cores
    hid = pltpu.VMEM((number, half_rows // number, cores * hidden_part), BF)
    mixed, fresh, first_new, second_new = pl.pallas_call(
        step_kernel,
        in_specs=[smem] * 4 + [vmem] * 7 + [hbm] * 5,
        out_specs=[vmem] * 4,
        out_shape=[
            jax.ShapeDtypeStruct((tok_rows, width), BF),
            jax.ShapeDtypeStruct((hidden_total, width), BF),
            jax.ShapeDtypeStruct((hidden_total, width), F32),
            jax.ShapeDtypeStruct((hidden_total, width), F32),
        ],
        scratch_shapes=[
            rows,
            rows,
            pltpu.VMEM((number,) + scale.shape, F32),
            state,
            state,
            state,
            state,
            state,
            rows,
            rows,
            state,
            state,
            state,
            state,
            state,
            state,
            hid,
            hid,
            hid,
            hid,
            rows,
            rows,
            pltpu.VMEM((parts, number // cores, slots, width), BF),
            pltpu.VMEM((cores, model_width, 2 * hidden_part), BF),
            pltpu.VMEM((model_width, hidden_part), BF),
            pltpu.VMEM((model_width, hidden_part), BF),
            pltpu.VMEM((parts, number, half_rows // number, cores * hidden_part), BF),
            pltpu.VMEM((hidden_total, width), F32),
            pltpu.VMEM((3, tok_rows, number * slots), BF),
            pltpu.SemaphoreType.DMA((KINDS,)),
            pltpu.SemaphoreType.DMA((KINDS,)),
            pltpu.SemaphoreType.DMA((KINDS,)),
            pltpu.SemaphoreType.DMA((4,)),
        ],
        compiler_params=pltpu.CompilerParams(
            collective_id=0, has_side_effects=True, vmem_limit_bytes=VMEM_LIMIT
        ),
        name="step",
    )(
        giver,
        my_giver,
        gate_scale.reshape(-1),
        up_scale.reshape(-1),
        old_expert.reshape(1, number),
        held.reshape(1, number),
        route_expert,
        route_weight,
        tokens,
        cotangent,
        scale,
        gate_quant[0],
        up_quant[0],
        down_quant.reshape(number, piece_rows, width),
        first_moment[0],
        second_moment[0],
    )
    return (mixed, fresh[None], first_new[None], second_new[None])


def solution(mesh):
    in_specs = (
        P("expert", "dp"),
        P("expert", None),
        P("expert", None),
        P("expert", "dp"),
        P("expert", None, "dp"),
        P("expert", None, "dp"),
        P("expert", None, "dp"),
        P("expert", None, "dp"),
        P("expert", None, "dp"),
        P("expert", None, "dp"),
        P("expert", None, "dp"),
        P("expert", None, "dp"),
        P(),
        P(),
    )
    out_specs = (
        P("expert", "dp"),
        P("expert", None, "dp"),
        P("expert", None, "dp"),
        P("expert", None, "dp"),
    )
    return jax.shard_map(
        per_device, mesh=mesh, in_specs=in_specs, out_specs=out_specs, check_vma=False
    )
```

```python
import jax
import jax.numpy as jnp
from jax import lax
from jax.experimental import pallas as pl
from jax.experimental.pallas import tpu as pltpu
from jax.sharding import PartitionSpec as P

QB = 128
BF = jnp.bfloat16
F32 = jnp.float32
MESH = pl.DeviceIdType.MESH

beta_first = 0.9
beta_second = 0.95
adam_eps = 1e-08
learn_rate = 0.003
decay_rate = 0.1
step_count = 20
fix_first = 1.0 - beta_first**step_count
fix_second = 1.0 - beta_second**step_count

VMEM_LIMIT = 58 * 1024 * 1024

T, SC, D1, F1, S1, D2, F2, S2, H1, H2, O, Y1, Y2, W, CX, CU = range(16)
KINDS = CU + 8


def transposed_dot(a, b):
    return lax.dot_general(a, b, (((0,), (0,)), ((), ())), preferred_element_type=F32)


def step_kernel(
    old_hbm,
    holder_hbm,
    gate_scale_hbm,
    up_scale_hbm,
    route_hbm,
    weight_hbm,
    tok_hbm,
    cot_hbm,
    scale_hbm,
    gate_hbm,
    up_hbm,
    down_hbm,
    first_hbm,
    second_hbm,
    grad_hbm,
    down_new_hbm,
    first_new,
    second_new,
    out_recv,
    pick_hbm,
    wide_hbm,
    old_ref,
    holder_ref,
    gate_scale_ref,
    up_scale_ref,
    route_ref,
    weight_ref,
    tok_ref,
    scale_ref,
    giver_ref,
    lanes_ref,
    tok_send,
    tok_recv,
    note_send,
    note_all,
    down_mid,
    first_send,
    first_mid,
    second_send,
    second_mid,
    cot_all,
    back_ref,
    down_out,
    down_new,
    first_out,
    second_out,
    hid_send,
    hid_mid,
    hid_out,
    hid_new,
    out_send,
    rows_all,
    weights_all,
    gate_v,
    up_v,
    hidden_all,
    grad_ref,
    pick_ref,
    wide_ref,
    send_sem,
    recv_sem,
    local_sem,
    load_sem,
):
    number = lax.axis_size("expert")
    parts = lax.axis_size("dp")
    cores = weights_all.shape[0]
    columns, depth = cot_all.shape[:2]
    e = lax.axis_index("expert")
    d = lax.axis_index("dp")
    core = lax.rem(d, cores)
    z = e // columns
    x = lax.rem(e, columns)
    tokens, width = tok_ref.shape
    slots = tok_send.shape[1]
    total = number * slots
    half = number // cores
    half_rows = half * slots
    hidden_part = gate_v.shape[1]

    def remote(src, dst, kind, target):
        return pltpu.make_async_remote_copy(
            src_ref=src,
            dst_ref=dst,
            send_sem=send_sem.at[kind],
            recv_sem=recv_sem.at[kind],
            device_id=target,
            device_id_type=MESH,
        )

    load_gate = pltpu.make_async_copy(gate_hbm, gate_v, load_sem.at[0])
    load_up = pltpu.make_async_copy(up_hbm, up_v, load_sem.at[1])
    load_first = pltpu.make_async_copy(first_hbm, grad_ref, load_sem.at[2])
    load_second = pltpu.make_async_copy(second_hbm, grad_ref, load_sem.at[3])
    small = [
        pltpu.make_async_copy(src, dst, load_sem.at[4 + i])
        for i, (src, dst) in enumerate(
            [
                (route_hbm, route_ref),
                (old_hbm, old_ref),
                (tok_hbm, tok_ref),
                (cot_hbm, cot_all.at[x, z]),
                (weight_hbm, weight_ref),
                (holder_hbm, holder_ref),
                (gate_scale_hbm, gate_scale_ref),
                (up_scale_hbm, up_scale_ref),
                (scale_hbm, scale_ref),
            ]
        )
    ]
    for load in small:
        load.start()
    load_gate.start()
    load_up.start()
    load_first.start()

    barrier = pltpu.get_barrier_semaphore()

    def greet_expert(k, carry):
        pl.semaphore_signal(
            barrier, inc=1, device_id=(lax.rem(e + k, number), d), device_id_type=MESH
        )
        return carry

    def greet_dp(k, carry):
        pl.semaphore_signal(
            barrier, inc=1, device_id=(e, lax.rem(d + k, parts)), device_id_type=MESH
        )
        return carry

    lax.fori_loop(1, number, greet_expert, 0)
    lax.fori_loop(1, parts, greet_dp, 0)

    i = lax.broadcasted_iota(jnp.int32, (tokens, tokens), 0)
    j = lax.broadcasted_iota(jnp.int32, (tokens, tokens), 1)
    earlier = (i < j).astype(BF)
    row = lax.broadcasted_iota(jnp.int32, (total, number), 0)
    holder = lax.broadcasted_iota(jnp.int32, (total, number), 1)
    spread = jnp.logical_and(row >= holder * slots, row < (holder + 1) * slots).astype(BF)
    place = lax.rem(lax.broadcasted_iota(jnp.int32, (total, tokens), 0), slots).astype(F32)
    label = lax.broadcasted_iota(jnp.int32, (number, tokens), 0)

    def ranks(hit):
        rank = jnp.dot(hit.astype(BF), earlier, preferred_element_type=F32)
        return jnp.where(hit > 0.0, rank, -1.0)

    def slot_hits(rank):
        return jnp.dot(spread, rank.astype(BF), preferred_element_type=F32) == place

    def experts_of(value_of):
        named = jnp.zeros((number, tokens), jnp.int32)
        for h in range(number):
            named = jnp.where(label == h, value_of(h), named)
        return named

    small[0].wait()
    small[1].wait()
    routes = route_ref[...]
    expert_before = experts_of(lambda h: old_ref[h])
    hit_before = jnp.zeros((number, tokens), F32)
    for k in range(routes.shape[0]):
        hit_before += (routes[k : k + 1, :] == expert_before).astype(F32)
    pick = slot_hits(ranks(hit_before)).astype(BF)
    small[2].wait()
    rows = jnp.dot(pick, tok_ref[...], preferred_element_type=F32)
    tok_send[...] = rows.astype(BF).reshape(tok_send.shape)

    pl.semaphore_wait(barrier, number - 1 + parts - 1)

    def send_all(src, dst, kind):
        def body(k, carry):
            t = lax.rem(e + k, number)
            remote(src.at[t], dst.at[e], kind, (t, d)).start()
            return carry

        lax.fori_loop(1, number, body, 0)
        pltpu.make_async_copy(src.at[e], dst.at[e], local_sem.at[kind]).start()

    def wait_all(src, dst, kind):
        rest = dst.at[pl.ds(0, number - 1)]
        remote(rest, rest, kind, (lax.rem(e + 1, number), d)).wait_recv()
        pltpu.make_async_copy(src.at[e], dst.at[e], local_sem.at[kind]).wait()

    def sent_all(dst, kind):
        rest = dst.at[pl.ds(0, number - 1)]
        remote(rest, rest, kind, (lax.rem(e + 1, number), d)).wait_send()

    def reorder(src, dst):
        def body(k, carry):
            dst[k] = src[giver_ref[k]]
            return carry

        lax.fori_loop(0, number, body, 0)

    send_all(tok_send, tok_recv, T)

    def ring(step, source, lines):
        above = (lax.rem(z + 1, depth) * columns + x, d)
        below = (lax.rem(z + depth - 1, depth) * columns + x, d)
        from_below = cot_all.at[x, lax.rem(z + depth - source, depth)]
        from_above = cot_all.at[x, lax.rem(z + source, depth)]
        if lines is not None:
            from_below = from_below.at[pl.ds(0, lines)]
            from_above = from_above.at[pl.ds(lines, lines)]
        up = remote(from_below, from_below, CU + 2 * step, above)
        down = remote(from_above, from_above, CU + 2 * step + 1, below)
        return up, down

    small[3].wait()
    rings = [ring(0, 0, None)]
    for copy in rings[0]:
        copy.start()

    load_gate.wait()
    load_up.wait()
    small[6].wait()
    small[7].wait()

    def dequantize(r, carry):
        lines = pl.ds(pl.multiple_of(r * QB, QB), QB)
        gate = (gate_v[lines, :].astype(F32) * gate_scale_ref[r]).astype(BF)
        up = (up_v[lines, :].astype(F32) * up_scale_ref[r]).astype(BF)
        weights_all[core, lines, :] = jnp.concatenate([gate, up], axis=1)
        return carry

    lax.fori_loop(0, gate_v.shape[0] // QB, dequantize, 0)
    sibling = (e, d + 1 - 2 * core)
    weights_copy = remote(weights_all.at[core], weights_all.at[core], W, sibling)
    weights_copy.start()

    for load in small[4:6] + small[8:]:
        load.wait()

    def forward(step, lines=None):
        for copy in rings[step - 1]:
            copy.wait_recv()
        rings.append(ring(step, step, lines))
        for copy in rings[step]:
            copy.start()

    forward(1)

    def find(h, carry):
        giver = jnp.int32(0)
        for g in range(number):
            giver = jnp.where(holder_ref[g] == h, g, giver)
        giver_ref[h] = giver
        return carry

    lax.fori_loop(0, number, find, 0)
    expert_after = experts_of(lambda h: old_ref[giver_ref[h]])
    hit_after = jnp.zeros((number, tokens), F32)
    weight_after = jnp.zeros((number, tokens), F32)
    for k in range(routes.shape[0]):
        match = routes[k : k + 1, :] == expert_after
        hit_after += match.astype(F32)
        weight_after += jnp.where(match, weight_ref[k : k + 1, :], 0.0)
    rank_after = ranks(hit_after)
    lanes_ref[...] = jnp.zeros_like(lanes_ref)
    lanes_ref[0, :, :tokens] = rank_after
    lanes_ref[1, :, :tokens] = weight_after
    note_rows, note_lanes = scale_ref.shape
    line = lax.broadcasted_iota(jnp.int32, (note_rows, note_lanes), 0)
    lane = lax.broadcasted_iota(jnp.int32, (note_rows, note_lanes), 1)
    for h in range(number):
        rank_row = jnp.broadcast_to(lanes_ref[0, h : h + 1, :], scale_ref.shape)
        weight_row = jnp.broadcast_to(lanes_ref[1, h : h + 1, :], scale_ref.shape)
        note = jnp.where(line == 0, rank_row, jnp.where(line == 1, weight_row, 0.0))
        note_send[h] = jnp.where(lane < tokens, note, scale_ref[...])
    send_all(note_send, note_all, SC)

    forward(2)
    load_first.wait()
    first_send[...] = grad_ref[...].astype(BF).reshape(first_send.shape)
    load_second.start()

    sent_all(tok_recv, T)
    send_all(down_hbm, down_mid, D1)

    hit_slots = slot_hits(rank_after)
    rest = weight_after
    for p in range(3):
        piece = rest.astype(BF)
        rest = rest - piece.astype(F32)
        wide = jnp.dot(spread, piece, preferred_element_type=F32)
        pick_ref[p] = jnp.where(hit_slots, wide, 0.0).astype(BF)
    forward(3, tokens // 2)
    load_second.wait()
    second_send[...] = grad_ref[...].astype(BF).reshape(second_send.shape)

    wait_all(tok_send, tok_recv, T)

    def send_rows(k, carry):
        t = lax.rem(d + k, parts)
        src = tok_recv.at[pl.ds(lax.rem(t, cores) * half, half)]
        remote(src, rows_all.at[d], Y1, (e, t)).start()
        return carry

    lax.fori_loop(1, parts, send_rows, 0)
    own_rows = pltpu.make_async_copy(
        tok_recv.at[pl.ds(core * half, half)], rows_all.at[d], local_sem.at[Y1]
    )
    own_rows.start()
    for copy in rings[3]:
        copy.wait_recv()

    def send_column(k, carry):
        t = (z * columns + lax.rem(x + k, columns), d)
        remote(cot_all.at[x], cot_all.at[x], CX, t).start()
        return carry

    lax.fori_loop(1, columns, send_column, 0)
    send_all(first_send, first_mid, F1)
    send_all(second_send, second_mid, S1)

    wait_all(down_hbm, down_mid, D1)
    reorder(down_mid, down_out)
    send_all(down_out, down_new, D2)

    own_rows.wait()
    weights_copy.wait()
    others = rows_all.at[pl.ds(0, parts - 1)]
    remote(others, others, Y1, sibling).wait()
    for c in range(cores):
        value = jnp.zeros((half_rows, 2 * hidden_part), F32)
        for k in range(parts):
            value += jnp.dot(
                rows_all[k].reshape(half_rows, width),
                weights_all[c, k * width : (k + 1) * width, :],
                preferred_element_type=F32,
            )
        gate = value[:, :hidden_part]
        up = value[:, hidden_part:]
        act = (gate / (1.0 + jnp.exp(-gate)) * up).astype(BF)
        hid_send[:, :, c * hidden_part : (c + 1) * hidden_part] = act.reshape(
            number, half_rows // number, hidden_part
        )
    send_all(hid_send, hid_mid, H1)

    wait_all(first_send, first_mid, F1)
    reorder(first_mid, first_out)
    send_all(first_out, first_new, F2)

    wait_all(hid_send, hid_mid, H1)
    reorder(hid_mid, hid_out)
    send_all(hid_out, hid_new, H2)

    wait_all(second_send, second_mid, S1)
    reorder(second_mid, second_out)
    send_all(second_out, second_new, S2)

    wait_all(hid_out, hid_new, H2)

    def send_hidden(k, carry):
        remote(hid_new, hidden_all.at[d], Y2, (e, lax.rem(d + k, parts))).start()
        return carry

    lax.fori_loop(1, parts, send_hidden, 0)
    own_hidden = pltpu.make_async_copy(hid_new, hidden_all.at[d], local_sem.at[Y2])
    own_hidden.start()

    wait_all(note_send, note_all, SC)
    wait_all(down_out, down_new, D2)
    save_down = pltpu.make_async_copy(down_new, down_new_hbm, load_sem.at[0])
    save_down.start()
    save_pick = pltpu.make_async_copy(pick_ref, pick_hbm, load_sem.at[1])
    save_pick.start()
    scale = note_all[giver_ref[e]]
    scale_wide = jnp.concatenate(
        [
            jnp.broadcast_to(scale[:, tokens + c : tokens + c + 1], (scale.shape[0], QB))
            for c in range(width // QB)
        ],
        axis=1,
    )
    wide_ref[...] = scale_wide
    save_wide = pltpu.make_async_copy(wide_ref, wide_hbm, load_sem.at[2])
    save_wide.start()
    pieces = QB // down_new.shape[1]

    def weight_rows(r):
        quant = down_new[r * pieces : (r + 1) * pieces].reshape(QB, width)
        return (quant.astype(F32) * scale_wide[r : r + 1, :]).astype(BF)

    own_hidden.wait()
    others = hidden_all.at[pl.ds(0, parts - 1)]
    remote(others, others, Y2, sibling).wait()
    pair = cores * hidden_part
    for c in range(cores):
        value = jnp.zeros((half_rows, width), F32)
        for y in range(parts // cores):
            down_w = jnp.concatenate(
                [weight_rows(y * pair // QB + r) for r in range(pair // QB)], axis=0
            )
            value += jnp.dot(
                hidden_all[y * cores + c].reshape(half_rows, pair),
                down_w,
                preferred_element_type=F32,
            )
        out_send[c * half : (c + 1) * half] = value.astype(BF).reshape(half, slots, width)
    send_all(out_send, out_recv, O)

    others = cot_all.at[pl.ds(0, columns - 1)]
    remote(others, others, CX, sibling).wait()
    for s in range(number):
        slot = lax.broadcasted_iota(jnp.int32, (slots, tokens), 0).astype(F32)
        hit = note_all[s, 0:1, :tokens] == slot
        weight = jnp.sum(jnp.where(hit, note_all[s, 1:2, :tokens], 0.0), axis=1, keepdims=True)
        block = cot_all[s % columns, s // columns]
        picked = jnp.dot(hit.astype(BF), block, preferred_element_type=F32)
        back_ref[s] = (weight * picked).astype(BF)

    for y in range(parts // cores):
        value = jnp.zeros((pair, width), F32)
        for c in range(cores):
            value += transposed_dot(
                hidden_all[y * cores + c].reshape(half_rows, pair),
                back_ref[c * half : (c + 1) * half].reshape(half_rows, width),
            )
        grad_ref[y * pair : (y + 1) * pair, :] = value
    save_grad = pltpu.make_async_copy(grad_ref, grad_hbm, load_sem.at[3])
    save_grad.start()

    for pair_of_copies in rings:
        for copy in pair_of_copies:
            copy.wait_send()
    for dst, kind in (
        (note_all, SC),
        (down_mid, D1),
        (first_mid, F1),
        (second_mid, S1),
        (down_new, D2),
        (first_new, F2),
        (second_new, S2),
        (hid_mid, H1),
        (hid_new, H2),
        (out_recv, O),
    ):
        sent_all(dst, kind)
    wait_all(first_out, first_new, F2)
    wait_all(second_out, second_new, S2)
    wait_all(out_send, out_recv, O)
    for save in (save_down, save_pick, save_wide, save_grad):
        save.wait()


def finish_kernel(
    grad_ref,
    down_ref,
    first_in,
    second_in,
    wide_ref,
    pick_ref,
    rows_ref,
    mixed_ref,
    fresh_ref,
    first_ref,
    second_ref,
):
    k = pl.program_id(0)
    tall, width = grad_ref.shape

    @pl.when(k == 0)
    def _():
        rows = rows_ref[...].reshape(-1, width)
        value = transposed_dot(pick_ref[0], rows)
        value += transposed_dot(pick_ref[1], rows)
        value += transposed_dot(pick_ref[2], rows)
        mixed_ref[...] = value.astype(BF)

    grad = grad_ref[...]
    quant = down_ref[...].reshape(tall, width).astype(F32)
    lines = tall // QB
    master = jnp.concatenate(
        [
            quant[r * QB : (r + 1) * QB, :] * wide_ref[pl.ds(k * lines + r, 1), :]
            for r in range(lines)
        ],
        axis=0,
    )
    first = first_in[...].reshape(tall, width).astype(F32)
    second = second_in[...].reshape(tall, width).astype(F32)
    first = beta_first * first + (1.0 - beta_first) * grad
    second = beta_second * second + (1.0 - beta_second) * grad * grad
    update = first / fix_first / (jnp.sqrt(second / fix_second) + adam_eps)
    fresh_ref[0] = (master - learn_rate * (update + decay_rate * master)).astype(BF)
    first_ref[0] = first
    second_ref[0] = second


def finish(grad, down_new, first_new, second_new, wide, pick, out_rows):
    hidden_total, width = grad.shape
    number, piece_rows, _ = down_new.shape
    tokens = pick.shape[2]
    steps = 4
    tall = hidden_total // steps
    state = pl.BlockSpec((number // steps, piece_rows, width), lambda k: (k, 0, 0))
    block = pl.BlockSpec((1, tall, width), lambda k: (0, k, 0))
    return pl.pallas_call(
        finish_kernel,
        grid=(steps,),
        in_specs=[
            pl.BlockSpec((tall, width), lambda k: (k, 0)),
            state,
            state,
            state,
            pl.BlockSpec(wide.shape, lambda k: (0, 0)),
            pl.BlockSpec(pick.shape, lambda k: (0, 0, 0)),
            pl.BlockSpec(out_rows.shape, lambda k: (0, 0, 0)),
        ],
        out_specs=[pl.BlockSpec((tokens, width), lambda k: (0, 0)), block, block, block],
        out_shape=[
            jax.ShapeDtypeStruct((tokens, width), BF),
            jax.ShapeDtypeStruct((1, hidden_total, width), BF),
            jax.ShapeDtypeStruct((1, hidden_total, width), F32),
            jax.ShapeDtypeStruct((1, hidden_total, width), F32),
        ],
        compiler_params=pltpu.CompilerParams(vmem_limit_bytes=VMEM_LIMIT),
        name="finish",
    )(grad, down_new, first_new, second_new, wide, pick, out_rows)


def per_device(
    tokens,
    route_weight,
    route_expert,
    cotangent,
    gate_quant,
    up_quant,
    gate_scale,
    up_scale,
    down_quant,
    down_scale,
    first_moment,
    second_moment,
    old_expert,
    new_holder,
):
    number = lax.axis_size("expert")
    parts = lax.axis_size("dp")
    cores = 2
    columns = 4
    tok_rows, top_count = route_expert.shape
    width = cotangent.shape[1]
    slots = min(tok_rows, tok_rows * top_count // number * 4 // 3)
    model_width, hidden_part = gate_quant.shape[1:]
    hidden_total = down_quant.shape[1]
    piece_rows = hidden_total // number
    scale_cols = down_scale.shape[2]
    scale = jnp.pad(down_scale[0], ((0, 0), (tok_rows, QB - tok_rows - scale_cols)))

    hbm = pl.BlockSpec(memory_space=pl.ANY)
    state_shape = (number, piece_rows, width)
    row_shape = (number, slots, width)
    pick_shape = (3, number * slots, tok_rows)
    wide_shape = (scale.shape[0], width)
    half_rows = number * slots // cores
    state = pltpu.VMEM(state_shape, BF)
    rows = pltpu.VMEM(row_shape, BF)
    note = pltpu.VMEM((number,) + scale.shape, F32)
    hid_shape = (number, half_rows // number, cores * hidden_part)
    hid = pltpu.VMEM(hid_shape, BF)
    parts_out = pl.pallas_call(
        step_kernel,
        in_specs=[hbm] * 14,
        out_specs=[hbm] * 7,
        out_shape=[
            jax.ShapeDtypeStruct((hidden_total, width), F32),
            jax.ShapeDtypeStruct(state_shape, BF),
            jax.ShapeDtypeStruct(state_shape, BF),
            jax.ShapeDtypeStruct(state_shape, BF),
            jax.ShapeDtypeStruct(row_shape, BF),
            jax.ShapeDtypeStruct(pick_shape, BF),
            jax.ShapeDtypeStruct(wide_shape, F32),
        ],
        scratch_shapes=[
            pltpu.SMEM((number,), jnp.int32),
            pltpu.SMEM((number,), jnp.int32),
            pltpu.SMEM((model_width // QB,), F32),
            pltpu.SMEM((model_width // QB,), F32),
            pltpu.VMEM((top_count, tok_rows), jnp.int32),
            pltpu.VMEM((top_count, tok_rows), F32),
            pltpu.VMEM((tok_rows, width), BF),
            pltpu.VMEM(scale.shape, F32),
            pltpu.SMEM((number,), jnp.int32),
            pltpu.VMEM((2, number, QB), F32),
            rows,
            rows,
            note,
            note,
            state,
            state,
            state,
            state,
            state,
            pltpu.VMEM((columns, number // columns, tok_rows, width), BF),
            rows,
            state,
            state,
            state,
            state,
            hid,
            hid,
            hid,
            hid,
            rows,
            pltpu.VMEM((parts, number // cores, slots, width), BF),
            pltpu.VMEM((cores, model_width, 2 * hidden_part), BF),
            pltpu.VMEM((model_width, hidden_part), BF),
            pltpu.VMEM((model_width, hidden_part), BF),
            pltpu.VMEM((parts,) + hid_shape, BF),
            pltpu.VMEM((hidden_total, width), F32),
            pltpu.VMEM(pick_shape, BF),
            pltpu.VMEM(wide_shape, F32),
            pltpu.SemaphoreType.DMA((KINDS,)),
            pltpu.SemaphoreType.DMA((KINDS,)),
            pltpu.SemaphoreType.DMA((KINDS,)),
            pltpu.SemaphoreType.DMA((13,)),
        ],
        compiler_params=pltpu.CompilerParams(
            collective_id=0, has_side_effects=True, vmem_limit_bytes=VMEM_LIMIT
        ),
        name="step",
    )(
        old_expert,
        new_holder,
        gate_scale.reshape(-1),
        up_scale.reshape(-1),
        route_expert.T,
        route_weight.T,
        tokens,
        cotangent,
        scale,
        gate_quant[0],
        up_quant[0],
        down_quant.reshape(state_shape),
        first_moment[0],
        second_moment[0],
    )
    grad, down_new, first_new, second_new, out_rows, pick, wide = parts_out
    return tuple(finish(grad, down_new, first_new, second_new, wide, pick, out_rows))


def solution(mesh):
    in_specs = (
        P("expert", "dp"),
        P("expert", None),
        P("expert", None),
        P("expert", "dp"),
        P("expert", None, "dp"),
        P("expert", None, "dp"),
        P("expert", None, "dp"),
        P("expert", None, "dp"),
        P("expert", None, "dp"),
        P("expert", None, "dp"),
        P("expert", None, "dp"),
        P("expert", None, "dp"),
        P(),
        P(),
    )
    out_specs = (
        P("expert", "dp"),
        P("expert", None, "dp"),
        P("expert", None, "dp"),
        P("expert", None, "dp"),
    )
    return jax.shard_map(
        per_device, mesh=mesh, in_specs=in_specs, out_specs=out_specs, check_vma=False
    )
```

```python
import jax
import jax.numpy as jnp
from jax import lax
from jax.experimental import pallas as pl
from jax.experimental.pallas import tpu as pltpu
from jax.sharding import PartitionSpec as P

QB = 128
BF = jnp.bfloat16
F32 = jnp.float32
MESH = pl.DeviceIdType.MESH

beta_first = 0.9
beta_second = 0.95
adam_eps = 1e-08
learn_rate = 0.003
decay_rate = 0.1
step_count = 20
fix_first = 1.0 - beta_first**step_count
fix_second = 1.0 - beta_second**step_count

VMEM_LIMIT = 58 * 1024 * 1024

SC, D1, F1, S1, D2, F2, S2, H1, H2, O, W, CX, TX, YS, YFU, YFD, Y2, Y3 = range(18)
YU = 18
YD = 20
TU = 22
CU = 30
TF = 38
CF = 40
TB = 42
CB = 43
KINDS = 44


def transposed_dot(a, b):
    return lax.dot_general(a, b, (((0,), (0,)), ((), ())), preferred_element_type=F32)


def step_kernel(
    old_hbm,
    holder_hbm,
    gate_scale_hbm,
    up_scale_hbm,
    route_hbm,
    weight_hbm,
    tok_hbm,
    cot_hbm,
    scale_hbm,
    gate_hbm,
    up_hbm,
    down_hbm,
    first_hbm,
    second_hbm,
    grad_hbm,
    down_new_hbm,
    first_new,
    second_new,
    out_recv,
    pick_hbm,
    wide_hbm,
    old_ref,
    holder_ref,
    gate_scale_ref,
    up_scale_ref,
    route_ref,
    weight_ref,
    scale_ref,
    giver_ref,
    lanes_ref,
    tok_all,
    tok_recv,
    note_send,
    note_all,
    down_mid,
    first_send,
    first_mid,
    second_send,
    second_mid,
    cot_all,
    back_ref,
    down_out,
    down_new,
    first_out,
    second_out,
    hid_send,
    hid_mid,
    hid_out,
    hid_new,
    out_send,
    rows_all,
    weights_all,
    gate_v,
    up_v,
    hidden_all,
    grad_ref,
    pick_ref,
    wide_ref,
    send_sem,
    recv_sem,
    local_sem,
    load_sem,
):
    number = lax.axis_size("expert")
    parts = lax.axis_size("dp")
    cores = weights_all.shape[0]
    columns, depth = cot_all.shape[:2]
    e = lax.axis_index("expert")
    d = lax.axis_index("dp")
    core = lax.rem(d, cores)
    z = e // columns
    x = lax.rem(e, columns)
    chip = d // cores
    chips = parts // cores
    tokens, width = tok_all.shape[2:]
    slots = tok_recv.shape[1]
    total = number * slots
    half = number // cores
    half_rows = half * slots
    hidden_part = gate_v.shape[1]

    def remote(src, dst, kind, target):
        return pltpu.make_async_remote_copy(
            src_ref=src,
            dst_ref=dst,
            send_sem=send_sem.at[kind],
            recv_sem=recv_sem.at[kind],
            device_id=target,
            device_id_type=MESH,
        )

    load_gate = pltpu.make_async_copy(gate_hbm, gate_v, load_sem.at[0])
    load_up = pltpu.make_async_copy(up_hbm, up_v, load_sem.at[1])
    load_first = pltpu.make_async_copy(first_hbm, grad_ref, load_sem.at[2])
    load_second = pltpu.make_async_copy(second_hbm, grad_ref, load_sem.at[3])
    small = [
        pltpu.make_async_copy(src, dst, load_sem.at[4 + i])
        for i, (src, dst) in enumerate(
            [
                (route_hbm, route_ref),
                (old_hbm, old_ref),
                (tok_hbm, tok_all.at[x, z]),
                (cot_hbm, cot_all.at[x, z]),
                (weight_hbm, weight_ref),
                (holder_hbm, holder_ref),
                (gate_scale_hbm, gate_scale_ref),
                (up_scale_hbm, up_scale_ref),
                (scale_hbm, scale_ref),
            ]
        )
    ]
    for load in small:
        load.start()
    load_gate.start()
    load_up.start()
    load_first.start()

    barrier = pltpu.get_barrier_semaphore()

    def greet_expert(k, carry):
        pl.semaphore_signal(
            barrier, inc=1, device_id=(lax.rem(e + k, number), d), device_id_type=MESH
        )
        return carry

    def greet_dp(k, carry):
        pl.semaphore_signal(
            barrier, inc=1, device_id=(e, lax.rem(d + k, parts)), device_id_type=MESH
        )
        return carry

    lax.fori_loop(1, number, greet_expert, 0)
    lax.fori_loop(1, parts, greet_dp, 0)

    def send_part(src, dst, kind, first, last):
        def body(k, carry):
            t = lax.rem(e + k, number)
            remote(src.at[t], dst.at[e], kind, (t, d)).start()
            return carry

        lax.fori_loop(first, last, body, 0)

    def send_all(src, dst, kind):
        send_part(src, dst, kind, 1, number)
        pltpu.make_async_copy(src.at[e], dst.at[e], local_sem.at[kind]).start()

    def wait_all(src, dst, kind):
        rest = dst.at[pl.ds(0, number - 1)]
        remote(rest, rest, kind, (lax.rem(e + 1, number), d)).wait_recv()
        pltpu.make_async_copy(src.at[e], dst.at[e], local_sem.at[kind]).wait()

    def sent_all(dst, kind):
        rest = dst.at[pl.ds(0, number - 1)]
        remote(rest, rest, kind, (lax.rem(e + 1, number), d)).wait_send()

    def reorder(src, dst):
        def body(k, carry):
            dst[k] = src[giver_ref[k]]
            return carry

        lax.fori_loop(0, number, body, 0)

    def ring(table, base, step):
        above = (lax.rem(z + 1, depth) * columns + x, d)
        below = (lax.rem(z + depth - 1, depth) * columns + x, d)
        from_below = table.at[x, lax.rem(z + depth - step, depth)]
        from_above = table.at[x, lax.rem(z + step, depth)]
        if step == depth // 2 - 1:
            lines = tokens // 2
            from_below = from_below.at[pl.ds(0, lines)]
            from_above = from_above.at[pl.ds(lines, lines)]
        up = remote(from_below, from_below, base + 2 * step, above)
        down = remote(from_above, from_above, base + 2 * step + 1, below)
        return up, down

    sibling = (e, d + 1 - 2 * core)
    right = (z * columns + lax.rem(x + 1, columns), d)
    left = (z * columns + lax.rem(x + columns - 1, columns), d)
    right_x, left_x = lax.rem(x + 1, columns), lax.rem(x + columns - 1, columns)

    def along_x(block, kinds):
        remote(block, block, kinds[0], right).start()
        remote(block, block, kinds[1], left).start()

    def pass_on(table, kinds, onward):
        copies = []
        for kind, k, source, low, target in (
            (kinds[0], onward, left_x, 0, right),
            (kinds[1], onward + 1, right_x, depth // 2, left),
        ):
            column = table.at[source]
            remote(column, column, kind, sibling).wait_recv()
            part = table.at[source, pl.ds(low, depth // 2)]
            copy = remote(part, part, k, target)
            copy.start()
            copies.append(copy)
        return copies

    token_rings = [ring(tok_all, TU, step) for step in range(depth // 2)]
    cot_rings = [ring(cot_all, CU, step) for step in range(depth // 2)]

    def start(copies):
        for copy in copies:
            copy.start()

    def arrive(copies):
        for copy in copies:
            copy.wait_recv()

    small[2].wait()
    pl.semaphore_wait(barrier, number - 1 + parts - 1)

    portion = number // 4
    start(token_rings[0])
    along_x(tok_all.at[x, z], (TX, TB))
    send_part(down_hbm, down_mid, D1, 1, portion)

    i = lax.broadcasted_iota(jnp.int32, (tokens, tokens), 0)
    j = lax.broadcasted_iota(jnp.int32, (tokens, tokens), 1)
    earlier = (i < j).astype(BF)
    label = lax.broadcasted_iota(jnp.int32, (number, tokens), 0)

    def ranks(hit):
        rank = jnp.dot(hit.astype(BF), earlier, preferred_element_type=F32)
        return jnp.where(hit > 0.0, rank, -1.0)

    small[0].wait()
    small[1].wait()
    small[4].wait()
    small[5].wait()
    small[8].wait()
    expert_before = jnp.zeros((number, tokens), jnp.int32)
    expert_after = jnp.zeros((number, tokens), jnp.int32)
    for h in range(number):
        expert_before = jnp.where(label == h, old_ref[h], expert_before)
        expert_after = jnp.where(label == holder_ref[h], old_ref[h], expert_after)
    routes = route_ref[...]
    hit_before = jnp.zeros((number, tokens), F32)
    hit_after = jnp.zeros((number, tokens), F32)
    weight_after = jnp.zeros((number, tokens), F32)
    for k in range(routes.shape[0]):
        hit_before += (routes[k : k + 1, :] == expert_before).astype(F32)
        match = routes[k : k + 1, :] == expert_after
        hit_after += match.astype(F32)
        weight_after += jnp.where(match, weight_ref[k : k + 1, :], 0.0)
    rank_after = ranks(hit_after)
    lanes_ref[...] = jnp.zeros_like(lanes_ref)
    lanes_ref[0, :, :tokens] = rank_after
    lanes_ref[1, :, :tokens] = weight_after
    lanes_ref[2, :, :tokens] = ranks(hit_before)
    note_shape = note_send.shape[1:]
    line = lax.broadcasted_iota(jnp.int32, note_shape, 0)
    lane = lax.broadcasted_iota(jnp.int32, note_shape, 1)
    for h in range(number):
        note = jnp.zeros(note_shape, F32)
        for r in range(3):
            spread_row = jnp.broadcast_to(lanes_ref[r, h : h + 1, :], note_shape)
            note = jnp.where(line == r, spread_row, note)
        note_send[h] = jnp.where(lane < tokens, note, scale_ref[...])
    send_all(note_send, note_all, SC)

    def ring_step(table, rings, step, kind):
        arrive(rings[step - 1])
        start(rings[step])
        along_x(table.at[x, lax.rem(z + depth - step, depth)], kind)
        along_x(table.at[x, lax.rem(z + step, depth)], kind)

    def ring_end(table, rings, kind):
        arrive(rings[-1])
        along_x(table.at[x, lax.rem(z + depth // 2, depth)], kind)

    ring_step(tok_all, token_rings, 1, (TX, TB))
    send_part(down_hbm, down_mid, D1, portion, 2 * portion)
    ring_step(tok_all, token_rings, 2, (TX, TB))
    send_part(down_hbm, down_mid, D1, 2 * portion, 3 * portion)
    ring_step(tok_all, token_rings, 3, (TX, TB))
    send_part(down_hbm, down_mid, D1, 3 * portion, number)
    pltpu.make_async_copy(down_hbm.at[e], down_mid.at[e], local_sem.at[D1]).start()

    load_first.wait()
    first_send[...] = grad_ref[...].astype(BF).reshape(first_send.shape)
    load_second.start()

    ring_end(tok_all, token_rings, (TX, TB))
    small[3].wait()
    start(cot_rings[0])
    send_all(first_send, first_mid, F1)

    load_gate.wait()
    load_up.wait()
    small[6].wait()
    small[7].wait()

    def dequantize(r, carry):
        lines = pl.ds(pl.multiple_of(r * QB, QB), QB)
        gate = (gate_v[lines, :].astype(F32) * gate_scale_ref[r]).astype(BF)
        up = (up_v[lines, :].astype(F32) * up_scale_ref[r]).astype(BF)
        weights_all[core, lines, :] = jnp.concatenate([gate, up], axis=1)
        return carry

    lax.fori_loop(0, gate_v.shape[0] // QB, dequantize, 0)
    weights_copy = remote(weights_all.at[core], weights_all.at[core], W, sibling)
    weights_copy.start()

    def find(h, carry):
        giver = jnp.int32(0)
        for g in range(number):
            giver = jnp.where(holder_ref[g] == h, g, giver)
        giver_ref[h] = giver
        return carry

    lax.fori_loop(0, number, find, 0)

    token_passed = pass_on(tok_all, (TX, TB), TF)
    wait_all(note_send, note_all, SC)
    for copy in token_passed:
        copy.wait_recv()
    slot = lax.broadcasted_iota(jnp.int32, (slots, tokens), 0).astype(F32)
    for s in range(number):
        hit = (note_all[s, 2:3, :tokens] == slot).astype(BF)
        block = tok_all[s % columns, s // columns]
        tok_recv[s] = jnp.dot(hit, block, preferred_element_type=F32).astype(BF)

    up_chip = lax.rem(chip + 1, chips) * cores
    down_chip = lax.rem(chip + chips - 1, chips) * cores
    for c in range(cores):
        src = tok_recv.at[pl.ds(c * half, half)]
        remote(src, rows_all.at[d], YU + core, (e, up_chip + c)).start()
        remote(src, rows_all.at[d], YD + core, (e, down_chip + c)).start()
    rows_sibling = remote(
        tok_recv.at[pl.ds((1 - core) * half, half)], rows_all.at[d], YS, sibling
    )
    rows_sibling.start()

    load_second.wait()
    second_send[...] = grad_ref[...].astype(BF).reshape(second_send.shape)
    arrive(cot_rings[0])
    start(cot_rings[1])
    send_all(second_send, second_mid, S1)
    wait_all(down_hbm, down_mid, D1)
    reorder(down_mid, down_out)
    send_all(down_out, down_new, D2)

    def row_chunk(k):
        return rows_all.at[k]

    def arrived(kind, k):
        remote(row_chunk(k), row_chunk(k), kind, sibling).wait_recv()

    arrived(YU, down_chip)
    pass_up = remote(row_chunk(down_chip), row_chunk(down_chip), YFU, (e, up_chip + core))
    pass_up.start()
    arrived(YD + 1, up_chip + 1)
    pass_down = remote(
        row_chunk(up_chip + 1), row_chunk(up_chip + 1), YFD, (e, down_chip + core)
    )
    pass_down.start()
    arrive(cot_rings[1])
    start(cot_rings[2])
    wait_all(first_send, first_mid, F1)
    reorder(first_mid, first_out)
    send_all(first_out, first_new, F2)
    arrive(cot_rings[2])
    start(cot_rings[3])

    rows_sibling.wait_recv()
    weights_copy.wait()
    arrived(YU + 1, down_chip + 1)
    arrived(YD, up_chip)
    far_chip = lax.rem(chip + 2, chips) * cores

    def partial(chunk, values):
        lines = pl.ds(pl.multiple_of(chunk * width, width), width)
        return [
            value
            + jnp.dot(chunk_rows, weights_all[c, lines, :], preferred_element_type=F32)
            for c, value in enumerate(values)
        ]

    values = [jnp.zeros((half_rows, 2 * hidden_part), F32) for _ in range(cores)]
    own = tok_recv[pl.ds(core * half, half)].reshape(half_rows, width)
    for chunk in (
        d,
        d + 1 - 2 * core,
        down_chip,
        down_chip + 1,
        up_chip,
        up_chip + 1,
        far_chip,
        far_chip + 1,
    ):
        if chunk is d:
            chunk_rows = own
        else:
            if chunk is far_chip:
                arrived(YFU, far_chip)
                arrived(YFD, far_chip + 1)
            chunk_rows = rows_all[chunk].reshape(half_rows, width)
        values = partial(chunk, values)
    for c, value in enumerate(values):
        gate = value[:, :hidden_part]
        up = value[:, hidden_part:]
        act = (gate / (1.0 + jnp.exp(-gate)) * up).astype(BF)
        hid_send[:, :, c * hidden_part : (c + 1) * hidden_part] = act.reshape(
            number, half_rows // number, hidden_part
        )
    send_all(hid_send, hid_mid, H1)
    arrive(cot_rings[-1])
    along_x(cot_all.at[x], (CX, CB))


    wait_all(hid_send, hid_mid, H1)
    reorder(hid_mid, hid_out)
    send_all(hid_out, hid_new, H2)
    wait_all(second_send, second_mid, S1)
    reorder(second_mid, second_out)
    send_all(second_out, second_new, S2)


    row = lax.broadcasted_iota(jnp.int32, (total, number), 0)
    holder = lax.broadcasted_iota(jnp.int32, (total, number), 1)
    spread = jnp.logical_and(row >= holder * slots, row < (holder + 1) * slots).astype(BF)
    place = lax.rem(lax.broadcasted_iota(jnp.int32, (total, tokens), 0), slots).astype(F32)
    wide_rank = jnp.dot(
        spread, lanes_ref[0, :, :tokens].astype(BF), preferred_element_type=F32
    )
    hit_slots = wide_rank == place
    rest = lanes_ref[1, :, :tokens]
    for p in range(pick_ref.shape[0]):
        piece = rest.astype(BF)
        rest = rest - piece.astype(F32)
        wide = jnp.dot(spread, piece, preferred_element_type=F32)
        pick_ref[p] = jnp.where(hit_slots, wide, 0.0).astype(BF)
    save_pick = pltpu.make_async_copy(pick_ref, pick_hbm, load_sem.at[1])
    save_pick.start()

    wait_all(hid_out, hid_new, H2)

    own_hidden = pltpu.make_async_copy(hid_new, hidden_all.at[d], local_sem.at[Y2])
    own_hidden.start()
    for k in range(1, chips):
        target = lax.rem(chip + k, chips) * cores + core
        remote(hid_new, hidden_all.at[d], Y2, (e, target)).start()
    remote(hid_new, hidden_all.at[d], Y3, sibling).start()

    others = hidden_all.at[pl.ds(0, chips - 1)]
    remote(others, others, Y2, sibling).wait_recv()
    for k in range(1, chips):
        chunk = hidden_all.at[lax.rem(chip + k, chips) * cores + core]
        remote(chunk, chunk, Y3, sibling).start()

    cot_passed = pass_on(cot_all, (CX, CB), CF)
    wait_all(down_out, down_new, D2)
    save_down = pltpu.make_async_copy(down_new, down_new_hbm, load_sem.at[0])
    save_down.start()
    scale = note_all[giver_ref[e]]
    scale_wide = jnp.concatenate(
        [
            jnp.concatenate(
                [
                    jnp.broadcast_to(scale[c : c + 1, tokens + r : tokens + r + 1], (1, QB))
                    for c in range(width // QB)
                ],
                axis=1,
            )
            for r in range(wide_ref.shape[0])
        ],
        axis=0,
    )
    wide_ref[...] = scale_wide
    save_wide = pltpu.make_async_copy(wide_ref, wide_hbm, load_sem.at[2])
    save_wide.start()
    pieces = QB // down_new.shape[1]

    def weight_rows(r):
        quant = down_new[r * pieces : (r + 1) * pieces].reshape(QB, width)
        return (quant.astype(F32) * scale_wide[r : r + 1, :]).astype(BF)

    own_hidden.wait()
    others = hidden_all.at[pl.ds(0, chips)]
    remote(others, others, Y3, sibling).wait_recv()
    pair = cores * hidden_part
    for c in range(cores):
        value = jnp.zeros((half_rows, width), F32)
        for y in range(chips):
            down_w = jnp.concatenate(
                [weight_rows(y * pair // QB + r) for r in range(pair // QB)], axis=0
            )
            value += jnp.dot(
                hidden_all[y * cores + c].reshape(half_rows, pair),
                down_w,
                preferred_element_type=F32,
            )
        out_send[c * half : (c + 1) * half] = value.astype(BF).reshape(half, slots, width)
    send_all(out_send, out_recv, O)

    for copy in cot_passed:
        copy.wait_recv()
    for s in range(number):
        hit = note_all[s, 0:1, :tokens] == slot
        weight = jnp.sum(jnp.where(hit, note_all[s, 1:2, :tokens], 0.0), axis=1, keepdims=True)
        block = cot_all[s % columns, s // columns]
        picked = jnp.dot(hit.astype(BF), block, preferred_element_type=F32)
        back_ref[s] = (weight * picked).astype(BF)
    for y in range(chips):
        value = jnp.zeros((pair, width), F32)
        for c in range(cores):
            value += transposed_dot(
                hidden_all[y * cores + c].reshape(half_rows, pair),
                back_ref[c * half : (c + 1) * half].reshape(half_rows, width),
            )
        grad_ref[y * pair : (y + 1) * pair, :] = value
    save_grad = pltpu.make_async_copy(grad_ref, grad_hbm, load_sem.at[3])
    save_grad.start()

    for copies in token_rings + cot_rings:
        for copy in copies:
            copy.wait_send()
    for table, kinds in ((tok_all, (TX, TB)), (cot_all, (CX, CB))):
        for kind in kinds:
            remote(table.at[0], table.at[0], kind, sibling).wait_send()
    for copy in token_passed + cot_passed:
        copy.wait_send()
    both = rows_all.at[pl.ds(0, cores)]
    remote(both, both, YU + core, sibling).wait_send()
    remote(both, both, YD + core, sibling).wait_send()
    rows_sibling.wait_send()
    pass_up.wait_send()
    pass_down.wait_send()
    others = hidden_all.at[pl.ds(0, chips - 1)]
    remote(others, others, Y2, sibling).wait_send()
    others = hidden_all.at[pl.ds(0, chips)]
    remote(others, others, Y3, sibling).wait_send()
    for dst, kind in (
        (note_all, SC),
        (down_mid, D1),
        (first_mid, F1),
        (second_mid, S1),
        (down_new, D2),
        (first_new, F2),
        (second_new, S2),
        (hid_mid, H1),
        (hid_new, H2),
        (out_recv, O),
    ):
        sent_all(dst, kind)
    wait_all(first_out, first_new, F2)
    wait_all(second_out, second_new, S2)
    wait_all(out_send, out_recv, O)
    for save in (save_down, save_pick, save_wide, save_grad):
        save.wait()


def finish_kernel(
    grad_ref,
    down_ref,
    first_in,
    second_in,
    wide_ref,
    pick_ref,
    rows_ref,
    mixed_ref,
    fresh_ref,
    first_ref,
    second_ref,
):
    k = pl.program_id(0)
    tall, width = grad_ref.shape

    @pl.when(k == 0)
    def _():
        rows = rows_ref[...].reshape(-1, width)
        value = transposed_dot(pick_ref[0], rows)
        value += transposed_dot(pick_ref[1], rows)
        mixed_ref[...] = value.astype(BF)

    grad = grad_ref[...]
    quant = down_ref[...].reshape(tall, width).astype(F32)
    lines = tall // QB
    master = jnp.concatenate(
        [
            quant[r * QB : (r + 1) * QB, :] * wide_ref[pl.ds(k * lines + r, 1), :]
            for r in range(lines)
        ],
        axis=0,
    )
    first = first_in[...].reshape(tall, width).astype(F32)
    second = second_in[...].reshape(tall, width).astype(F32)
    first = beta_first * first + (1.0 - beta_first) * grad
    second = beta_second * second + (1.0 - beta_second) * grad * grad
    update = first / fix_first / (jnp.sqrt(second / fix_second) + adam_eps)
    fresh_ref[0] = (master - learn_rate * (update + decay_rate * master)).astype(BF)
    first_ref[0] = first
    second_ref[0] = second


def finish(grad, down_new, first_new, second_new, wide, pick, out_rows):
    hidden_total, width = grad.shape
    number, piece_rows, _ = down_new.shape
    tokens = pick.shape[2]
    steps = 2
    tall = hidden_total // steps
    state = pl.BlockSpec((number // steps, piece_rows, width), lambda k: (k, 0, 0))
    block = pl.BlockSpec((1, tall, width), lambda k: (0, k, 0))
    return pl.pallas_call(
        finish_kernel,
        grid=(steps,),
        in_specs=[
            pl.BlockSpec((tall, width), lambda k: (k, 0)),
            state,
            state,
            state,
            pl.BlockSpec(wide.shape, lambda k: (0, 0)),
            pl.BlockSpec(pick.shape, lambda k: (0, 0, 0)),
            pl.BlockSpec(out_rows.shape, lambda k: (0, 0, 0)),
        ],
        out_specs=[pl.BlockSpec((tokens, width), lambda k: (0, 0)), block, block, block],
        out_shape=[
            jax.ShapeDtypeStruct((tokens, width), BF),
            jax.ShapeDtypeStruct((1, hidden_total, width), BF),
            jax.ShapeDtypeStruct((1, hidden_total, width), F32),
            jax.ShapeDtypeStruct((1, hidden_total, width), F32),
        ],
        compiler_params=pltpu.CompilerParams(vmem_limit_bytes=VMEM_LIMIT),
        name="finish",
    )(grad, down_new, first_new, second_new, wide, pick, out_rows)


def per_device(
    tokens,
    route_weight,
    route_expert,
    cotangent,
    gate_quant,
    up_quant,
    gate_scale,
    up_scale,
    down_quant,
    down_scale,
    first_moment,
    second_moment,
    old_expert,
    new_holder,
):
    number = lax.axis_size("expert")
    parts = lax.axis_size("dp")
    cores = 2
    columns = 4
    tok_rows, top_count = route_expert.shape
    width = cotangent.shape[1]
    slots = min(tok_rows, tok_rows * top_count // number * 4 // 3)
    model_width, hidden_part = gate_quant.shape[1:]
    hidden_total = down_quant.shape[1]
    piece_rows = hidden_total // number
    scale = jnp.pad(
        down_scale[0].T, ((0, 0), (tok_rows, QB - tok_rows - hidden_total // QB))
    )

    hbm = pl.BlockSpec(memory_space=pl.ANY)
    state_shape = (number, piece_rows, width)
    row_shape = (number, slots, width)
    pick_shape = (2, number * slots, tok_rows)
    wide_shape = (hidden_total // QB, width)
    half_rows = number * slots // cores
    state = pltpu.VMEM(state_shape, BF)
    rows = pltpu.VMEM(row_shape, BF)
    note = pltpu.VMEM((number,) + scale.shape, F32)
    hid_shape = (number, half_rows // number, cores * hidden_part)
    hid = pltpu.VMEM(hid_shape, BF)
    parts_out = pl.pallas_call(
        step_kernel,
        in_specs=[hbm] * 14,
        out_specs=[hbm] * 7,
        out_shape=[
            jax.ShapeDtypeStruct((hidden_total, width), F32),
            jax.ShapeDtypeStruct(state_shape, BF),
            jax.ShapeDtypeStruct(state_shape, BF),
            jax.ShapeDtypeStruct(state_shape, BF),
            jax.ShapeDtypeStruct(row_shape, BF),
            jax.ShapeDtypeStruct(pick_shape, BF),
            jax.ShapeDtypeStruct(wide_shape, F32),
        ],
        scratch_shapes=[
            pltpu.SMEM((number,), jnp.int32),
            pltpu.SMEM((number,), jnp.int32),
            pltpu.SMEM((model_width // QB,), F32),
            pltpu.SMEM((model_width // QB,), F32),
            pltpu.VMEM((top_count, tok_rows), jnp.int32),
            pltpu.VMEM((top_count, tok_rows), F32),
            pltpu.VMEM(scale.shape, F32),
            pltpu.SMEM((number,), jnp.int32),
            pltpu.VMEM((3, number, QB), F32),
            pltpu.VMEM((columns, number // columns, tok_rows, width), BF),
            rows,
            note,
            note,
            state,
            state,
            state,
            state,
            state,
            pltpu.VMEM((columns, number // columns, tok_rows, width), BF),
            rows,
            state,
            state,
            state,
            state,
            hid,
            hid,
            hid,
            hid,
            rows,
            pltpu.VMEM((parts, number // cores, slots, width), BF),
            pltpu.VMEM((cores, model_width, 2 * hidden_part), BF),
            pltpu.VMEM((model_width, hidden_part), BF),
            pltpu.VMEM((model_width, hidden_part), BF),
            pltpu.VMEM((parts,) + hid_shape, BF),
            pltpu.VMEM((hidden_total, width), F32),
            pltpu.VMEM(pick_shape, BF),
            pltpu.VMEM(wide_shape, F32),
            pltpu.SemaphoreType.DMA((KINDS,)),
            pltpu.SemaphoreType.DMA((KINDS,)),
            pltpu.SemaphoreType.DMA((KINDS,)),
            pltpu.SemaphoreType.DMA((13,)),
        ],
        compiler_params=pltpu.CompilerParams(
            collective_id=0, has_side_effects=True, vmem_limit_bytes=VMEM_LIMIT
        ),
        name="step",
    )(
        old_expert,
        new_holder,
        gate_scale.reshape(-1),
        up_scale.reshape(-1),
        route_expert.T,
        route_weight.T,
        tokens,
        cotangent,
        scale,
        gate_quant[0],
        up_quant[0],
        down_quant.reshape(state_shape),
        first_moment[0],
        second_moment[0],
    )
    grad, down_new, first_new, second_new, out_rows, pick, wide = parts_out
    return tuple(finish(grad, down_new, first_new, second_new, wide, pick, out_rows))


def solution(mesh):
    in_specs = (
        P("expert", "dp"),
        P("expert", None),
        P("expert", None),
        P("expert", "dp"),
        P("expert", None, "dp"),
        P("expert", None, "dp"),
        P("expert", None, "dp"),
        P("expert", None, "dp"),
        P("expert", None, "dp"),
        P("expert", None, "dp"),
        P("expert", None, "dp"),
        P("expert", None, "dp"),
        P(),
        P(),
    )
    out_specs = (
        P("expert", "dp"),
        P("expert", None, "dp"),
        P("expert", None, "dp"),
        P("expert", None, "dp"),
    )
    return jax.shard_map(
        per_device, mesh=mesh, in_specs=in_specs, out_specs=out_specs, check_vma=False
    )
```

```python
import jax
import jax.numpy as jnp
from jax import lax
from jax.experimental import pallas as pl
from jax.experimental.pallas import tpu as pltpu
from jax.sharding import PartitionSpec as P

QB = 128
BF = jnp.bfloat16
F32 = jnp.float32
MESH = pl.DeviceIdType.MESH

beta_first = 0.9
beta_second = 0.95
adam_eps = 1e-08
learn_rate = 0.003
decay_rate = 0.1
step_count = 20
fix_first = 1.0 - beta_first**step_count
fix_second = 1.0 - beta_second**step_count

VMEM_LIMIT = 58 * 1024 * 1024

SC, D1, F1, S1, D2, F2, S2, H1, H2, O, W, CX, TX, YS, YFU, YFD, Y2, Y3 = range(18)
YU = 18
YD = 20
TU = 22
CU = 30
TF = 38
CF = 40
TB = 42
CB = 43
KINDS = 44


def transposed_dot(a, b):
    return lax.dot_general(a, b, (((0,), (0,)), ((), ())), preferred_element_type=F32)


def step_kernel(
    old_hbm,
    holder_hbm,
    gate_scale_hbm,
    up_scale_hbm,
    route_hbm,
    weight_hbm,
    tok_hbm,
    cot_hbm,
    scale_hbm,
    gate_hbm,
    up_hbm,
    down_hbm,
    first_hbm,
    second_hbm,
    grad_hbm,
    down_new_hbm,
    first_new,
    second_new,
    out_recv,
    pick_hbm,
    wide_hbm,
    old_ref,
    holder_ref,
    gate_scale_ref,
    up_scale_ref,
    route_ref,
    weight_ref,
    scale_ref,
    scale_lanes,
    giver_ref,
    lanes_ref,
    tok_all,
    tok_recv,
    note_send,
    note_all,
    down_mid,
    first_send,
    first_mid,
    second_send,
    second_mid,
    cot_all,
    back_ref,
    down_out,
    down_new,
    first_out,
    second_out,
    hid_send,
    hid_mid,
    hid_out,
    hid_new,
    out_send,
    rows_all,
    weights_all,
    gate_v,
    up_v,
    hidden_all,
    grad_ref,
    pick_ref,
    wide_ref,
    send_sem,
    recv_sem,
    local_sem,
    load_sem,
):
    number = lax.axis_size("expert")
    parts = lax.axis_size("dp")
    cores = weights_all.shape[0]
    columns, depth = cot_all.shape[:2]
    e = lax.axis_index("expert")
    d = lax.axis_index("dp")
    core = lax.rem(d, cores)
    z = e // columns
    x = lax.rem(e, columns)
    chip = d // cores
    chips = parts // cores
    tokens, width = tok_all.shape[2:]
    slots = tok_recv.shape[1]
    total = number * slots
    half = number // cores
    half_rows = half * slots
    hidden_part = gate_v.shape[1]

    def remote(src, dst, kind, target):
        return pltpu.make_async_remote_copy(
            src_ref=src,
            dst_ref=dst,
            send_sem=send_sem.at[kind],
            recv_sem=recv_sem.at[kind],
            device_id=target,
            device_id_type=MESH,
        )

    load_gate = pltpu.make_async_copy(gate_hbm, gate_v, load_sem.at[0])
    load_up = pltpu.make_async_copy(up_hbm, up_v, load_sem.at[1])
    load_first = pltpu.make_async_copy(first_hbm, grad_ref, load_sem.at[2])
    load_second = pltpu.make_async_copy(second_hbm, grad_ref, load_sem.at[3])
    small = [
        pltpu.make_async_copy(src, dst, load_sem.at[4 + i])
        for i, (src, dst) in enumerate(
            [
                (route_hbm, route_ref),
                (old_hbm, old_ref),
                (tok_hbm, tok_all.at[x, z]),
                (cot_hbm, cot_all.at[x, z]),
                (weight_hbm, weight_ref),
                (holder_hbm, holder_ref),
                (gate_scale_hbm, gate_scale_ref),
                (up_scale_hbm, up_scale_ref),
                (scale_hbm, scale_ref),
            ]
        )
    ]
    for load in small:
        load.start()
    load_gate.start()
    load_up.start()
    load_first.start()

    barrier = pltpu.get_barrier_semaphore()

    def greet_expert(k, carry):
        pl.semaphore_signal(
            barrier, inc=1, device_id=(lax.rem(e + k, number), d), device_id_type=MESH
        )
        return carry

    def greet_dp(k, carry):
        pl.semaphore_signal(
            barrier, inc=1, device_id=(e, lax.rem(d + k, parts)), device_id_type=MESH
        )
        return carry

    lax.fori_loop(1, number, greet_expert, 0)
    lax.fori_loop(1, parts, greet_dp, 0)

    def send_part(src, dst, kind, first, last):
        def body(k, carry):
            t = lax.rem(e + k, number)
            remote(src.at[t], dst.at[e], kind, (t, d)).start()
            return carry

        lax.fori_loop(first, last, body, 0)

    def send_all(src, dst, kind):
        send_part(src, dst, kind, 1, number)
        pltpu.make_async_copy(src.at[e], dst.at[e], local_sem.at[kind]).start()

    def wait_all(src, dst, kind):
        rest = dst.at[pl.ds(0, number - 1)]
        remote(rest, rest, kind, (lax.rem(e + 1, number), d)).wait_recv()
        pltpu.make_async_copy(src.at[e], dst.at[e], local_sem.at[kind]).wait()

    def sent_all(dst, kind):
        rest = dst.at[pl.ds(0, number - 1)]
        remote(rest, rest, kind, (lax.rem(e + 1, number), d)).wait_send()

    def reorder(src, dst):
        def body(k, carry):
            dst[k] = src[giver_ref[k]]
            return carry

        lax.fori_loop(0, number, body, 0)

    def ring(table, base, step):
        above = (lax.rem(z + 1, depth) * columns + x, d)
        below = (lax.rem(z + depth - 1, depth) * columns + x, d)
        from_below = table.at[x, lax.rem(z + depth - step, depth)]
        from_above = table.at[x, lax.rem(z + step, depth)]
        if step == depth // 2 - 1:
            lines = tokens // 2
            from_below = from_below.at[pl.ds(0, lines)]
            from_above = from_above.at[pl.ds(lines, lines)]
        up = remote(from_below, from_below, base + 2 * step, above)
        down = remote(from_above, from_above, base + 2 * step + 1, below)
        return up, down

    sibling = (e, d + 1 - 2 * core)
    right = (z * columns + lax.rem(x + 1, columns), d)
    left = (z * columns + lax.rem(x + columns - 1, columns), d)
    right_x, left_x = lax.rem(x + 1, columns), lax.rem(x + columns - 1, columns)

    def along_x(block, kinds):
        remote(block, block, kinds[0], right).start()
        remote(block, block, kinds[1], left).start()

    def pass_on(table, kinds, onward):
        copies = []
        for kind, k, source, low, target in (
            (kinds[0], onward, left_x, 0, right),
            (kinds[1], onward + 1, right_x, depth // 2, left),
        ):
            column = table.at[source]
            remote(column, column, kind, sibling).wait_recv()
            part = table.at[source, pl.ds(low, depth // 2)]
            copy = remote(part, part, k, target)
            copy.start()
            copies.append(copy)
        return copies

    token_rings = [ring(tok_all, TU, step) for step in range(depth // 2)]
    cot_rings = [ring(cot_all, CU, step) for step in range(depth // 2)]

    def start(copies):
        for copy in copies:
            copy.start()

    def arrive(copies):
        for copy in copies:
            copy.wait_recv()

    small[2].wait()
    pl.semaphore_wait(barrier, number - 1 + parts - 1)

    portion = number // 4
    start(token_rings[0])
    along_x(tok_all.at[x, z], (TX, TB))
    send_part(down_hbm, down_mid, D1, 1, portion)

    i = lax.broadcasted_iota(jnp.int32, (tokens, tokens), 0)
    j = lax.broadcasted_iota(jnp.int32, (tokens, tokens), 1)
    earlier = (i < j).astype(BF)
    label = lax.broadcasted_iota(jnp.int32, (number, tokens), 0)

    def ranks(hit):
        rank = jnp.dot(hit.astype(BF), earlier, preferred_element_type=F32)
        return jnp.where(hit > 0.0, rank, -1.0)

    small[0].wait()
    small[1].wait()
    small[4].wait()
    small[5].wait()
    small[8].wait()
    expert_before = jnp.zeros((number, tokens), jnp.int32)
    expert_after = jnp.zeros((number, tokens), jnp.int32)
    for h in range(number):
        expert_before = jnp.where(label == h, old_ref[h], expert_before)
        expert_after = jnp.where(label == holder_ref[h], old_ref[h], expert_after)
    routes = route_ref[...]
    hit_before = jnp.zeros((number, tokens), F32)
    hit_after = jnp.zeros((number, tokens), F32)
    weight_after = jnp.zeros((number, tokens), F32)
    for k in range(routes.shape[0]):
        hit_before += (routes[k : k + 1, :] == expert_before).astype(F32)
        match = routes[k : k + 1, :] == expert_after
        hit_after += match.astype(F32)
        weight_after += jnp.where(match, weight_ref[k : k + 1, :], 0.0)
    rank_after = ranks(hit_after)
    lanes_ref[...] = jnp.zeros_like(lanes_ref)
    lanes_ref[0, :, :tokens] = rank_after
    lanes_ref[1, :, :tokens] = weight_after
    lanes_ref[2, :, :tokens] = ranks(hit_before)
    scale_lanes[...] = jnp.zeros_like(scale_lanes)
    scale_lanes[: scale_ref.shape[0], : scale_ref.shape[1]] = scale_ref[...]
    scale_note = pltpu.roll(scale_lanes[...], tokens, 1)[: scale_ref.shape[0], :]
    note_shape = note_send.shape[1:]
    line = lax.broadcasted_iota(jnp.int32, note_shape, 0)
    lane = lax.broadcasted_iota(jnp.int32, note_shape, 1)
    for h in range(number):
        note = jnp.zeros(note_shape, F32)
        for r in range(3):
            spread_row = jnp.broadcast_to(lanes_ref[r, h : h + 1, :], note_shape)
            note = jnp.where(line == r, spread_row, note)
        note_send[h] = jnp.where(lane < tokens, note, scale_note)
    send_all(note_send, note_all, SC)

    def ring_step(table, rings, step, kind):
        arrive(rings[step - 1])
        start(rings[step])
        along_x(table.at[x, lax.rem(z + depth - step, depth)], kind)
        along_x(table.at[x, lax.rem(z + step, depth)], kind)

    def ring_end(table, rings, kind):
        arrive(rings[-1])
        along_x(table.at[x, lax.rem(z + depth // 2, depth)], kind)

    ring_step(tok_all, token_rings, 1, (TX, TB))
    send_part(down_hbm, down_mid, D1, portion, 2 * portion)
    ring_step(tok_all, token_rings, 2, (TX, TB))
    send_part(down_hbm, down_mid, D1, 2 * portion, 3 * portion)
    ring_step(tok_all, token_rings, 3, (TX, TB))
    send_part(down_hbm, down_mid, D1, 3 * portion, number)
    pltpu.make_async_copy(down_hbm.at[e], down_mid.at[e], local_sem.at[D1]).start()

    load_first.wait()
    first_send[...] = grad_ref[...].astype(BF).reshape(first_send.shape)
    load_second.start()

    ring_end(tok_all, token_rings, (TX, TB))
    small[3].wait()
    start(cot_rings[0])
    send_all(first_send, first_mid, F1)

    load_gate.wait()
    load_up.wait()
    small[6].wait()
    small[7].wait()

    def dequantize(r, carry):
        lines = pl.ds(pl.multiple_of(r * QB, QB), QB)
        gate = (gate_v[lines, :].astype(F32) * gate_scale_ref[r]).astype(BF)
        up = (up_v[lines, :].astype(F32) * up_scale_ref[r]).astype(BF)
        weights_all[core, lines, :] = jnp.concatenate([gate, up], axis=1)
        return carry

    lax.fori_loop(0, gate_v.shape[0] // QB, dequantize, 0)
    weights_copy = remote(weights_all.at[core], weights_all.at[core], W, sibling)
    weights_copy.start()

    def find(h, carry):
        giver = jnp.int32(0)
        for g in range(number):
            giver = jnp.where(holder_ref[g] == h, g, giver)
        giver_ref[h] = giver
        return carry

    lax.fori_loop(0, number, find, 0)

    token_passed = pass_on(tok_all, (TX, TB), TF)
    wait_all(note_send, note_all, SC)
    for copy in token_passed:
        copy.wait_recv()
    slot = lax.broadcasted_iota(jnp.int32, (slots, tokens), 0).astype(F32)
    for s in range(number):
        hit = (note_all[s, 2:3, :tokens] == slot).astype(BF)
        block = tok_all[s % columns, s // columns]
        tok_recv[s] = jnp.dot(hit, block, preferred_element_type=F32).astype(BF)

    up_chip = lax.rem(chip + 1, chips) * cores
    down_chip = lax.rem(chip + chips - 1, chips) * cores
    for c in range(cores):
        src = tok_recv.at[pl.ds(c * half, half)]
        remote(src, rows_all.at[d], YU + core, (e, up_chip + c)).start()
        remote(src, rows_all.at[d], YD + core, (e, down_chip + c)).start()
    rows_sibling = remote(
        tok_recv.at[pl.ds((1 - core) * half, half)], rows_all.at[d], YS, sibling
    )
    rows_sibling.start()

    load_second.wait()
    second_send[...] = grad_ref[...].astype(BF).reshape(second_send.shape)
    arrive(cot_rings[0])
    start(cot_rings[1])
    send_all(second_send, second_mid, S1)
    wait_all(down_hbm, down_mid, D1)
    reorder(down_mid, down_out)
    send_all(down_out, down_new, D2)

    def row_chunk(k):
        return rows_all.at[k]

    def arrived(kind, k):
        remote(row_chunk(k), row_chunk(k), kind, sibling).wait_recv()

    arrived(YU, down_chip)
    pass_up = remote(row_chunk(down_chip), row_chunk(down_chip), YFU, (e, up_chip + core))
    pass_up.start()
    arrived(YD + 1, up_chip + 1)
    pass_down = remote(
        row_chunk(up_chip + 1), row_chunk(up_chip + 1), YFD, (e, down_chip + core)
    )
    pass_down.start()
    arrive(cot_rings[1])
    start(cot_rings[2])
    arrive(cot_rings[2])
    start(cot_rings[3])

    rows_sibling.wait_recv()
    weights_copy.wait()
    arrived(YU + 1, down_chip + 1)
    arrived(YD, up_chip)
    far_chip = lax.rem(chip + 2, chips) * cores

    def partial(chunk, values):
        lines = pl.ds(pl.multiple_of(chunk * width, width), width)
        return [
            value
            + jnp.dot(chunk_rows, weights_all[c, lines, :], preferred_element_type=F32)
            for c, value in enumerate(values)
        ]

    values = [jnp.zeros((half_rows, 2 * hidden_part), F32) for _ in range(cores)]
    own = tok_recv[pl.ds(core * half, half)].reshape(half_rows, width)
    for chunk in (
        d,
        d + 1 - 2 * core,
        down_chip,
        down_chip + 1,
        up_chip,
        up_chip + 1,
        far_chip,
        far_chip + 1,
    ):
        if chunk is d:
            chunk_rows = own
        else:
            if chunk is far_chip:
                arrived(YFU, far_chip)
                arrived(YFD, far_chip + 1)
            chunk_rows = rows_all[chunk].reshape(half_rows, width)
        values = partial(chunk, values)
    for c, value in enumerate(values):
        gate = value[:, :hidden_part]
        up = value[:, hidden_part:]
        act = (gate / (1.0 + jnp.exp(-gate)) * up).astype(BF)
        hid_send[:, :, c * hidden_part : (c + 1) * hidden_part] = act.reshape(
            number, half_rows // number, hidden_part
        )
    send_all(hid_send, hid_mid, H1)
    wait_all(first_send, first_mid, F1)
    reorder(first_mid, first_out)
    send_part(first_out, first_new, F2, 1, number // 2)
    arrive(cot_rings[-1])
    along_x(cot_all.at[x], (CX, CB))


    wait_all(hid_send, hid_mid, H1)
    reorder(hid_mid, hid_out)
    send_all(hid_out, hid_new, H2)
    send_part(first_out, first_new, F2, number // 2, number)
    pltpu.make_async_copy(first_out.at[e], first_new.at[e], local_sem.at[F2]).start()
    wait_all(second_send, second_mid, S1)
    reorder(second_mid, second_out)
    send_all(second_out, second_new, S2)


    row = lax.broadcasted_iota(jnp.int32, (total, number), 0)
    holder = lax.broadcasted_iota(jnp.int32, (total, number), 1)
    spread = jnp.logical_and(row >= holder * slots, row < (holder + 1) * slots).astype(BF)
    place = lax.rem(lax.broadcasted_iota(jnp.int32, (total, tokens), 0), slots).astype(F32)
    wide_rank = jnp.dot(
        spread, lanes_ref[0, :, :tokens].astype(BF), preferred_element_type=F32
    )
    hit_slots = wide_rank == place
    rest = lanes_ref[1, :, :tokens]
    for p in range(pick_ref.shape[0]):
        piece = rest.astype(BF)
        rest = rest - piece.astype(F32)
        wide = jnp.dot(spread, piece, preferred_element_type=F32)
        pick_ref[p] = jnp.where(hit_slots, wide, 0.0).astype(BF)
    save_pick = pltpu.make_async_copy(pick_ref, pick_hbm, load_sem.at[1])
    save_pick.start()

    wait_all(hid_out, hid_new, H2)

    own_hidden = pltpu.make_async_copy(hid_new, hidden_all.at[d], local_sem.at[Y2])
    own_hidden.start()
    for k in range(1, chips):
        target = lax.rem(chip + k, chips) * cores + core
        remote(hid_new, hidden_all.at[d], Y2, (e, target)).start()
    remote(hid_new, hidden_all.at[d], Y3, sibling).start()

    others = hidden_all.at[pl.ds(0, chips - 1)]
    remote(others, others, Y2, sibling).wait_recv()
    for k in range(1, chips):
        chunk = hidden_all.at[lax.rem(chip + k, chips) * cores + core]
        remote(chunk, chunk, Y3, sibling).start()

    cot_passed = pass_on(cot_all, (CX, CB), CF)
    wait_all(down_out, down_new, D2)
    save_down = pltpu.make_async_copy(down_new, down_new_hbm, load_sem.at[0])
    save_down.start()
    scale = note_all[giver_ref[e]]
    scale_wide = jnp.concatenate(
        [
            jnp.concatenate(
                [
                    jnp.broadcast_to(scale[c : c + 1, tokens + r : tokens + r + 1], (1, QB))
                    for c in range(width // QB)
                ],
                axis=1,
            )
            for r in range(wide_ref.shape[0])
        ],
        axis=0,
    )
    wide_ref[...] = scale_wide
    save_wide = pltpu.make_async_copy(wide_ref, wide_hbm, load_sem.at[2])
    save_wide.start()
    pieces = QB // down_new.shape[1]

    def weight_rows(r):
        quant = down_new[r * pieces : (r + 1) * pieces].reshape(QB, width)
        return (quant.astype(F32) * scale_wide[r : r + 1, :]).astype(BF)

    own_hidden.wait()
    others = hidden_all.at[pl.ds(0, chips)]
    remote(others, others, Y3, sibling).wait_recv()
    pair = cores * hidden_part
    for c in range(cores):
        value = jnp.zeros((half_rows, width), F32)
        for y in range(chips):
            down_w = jnp.concatenate(
                [weight_rows(y * pair // QB + r) for r in range(pair // QB)], axis=0
            )
            value += jnp.dot(
                hidden_all[y * cores + c].reshape(half_rows, pair),
                down_w,
                preferred_element_type=F32,
            )
        out_send[c * half : (c + 1) * half] = value.astype(BF).reshape(half, slots, width)
    send_all(out_send, out_recv, O)

    for copy in cot_passed:
        copy.wait_recv()
    for s in range(number):
        hit = note_all[s, 0:1, :tokens] == slot
        weight = jnp.sum(jnp.where(hit, note_all[s, 1:2, :tokens], 0.0), axis=1, keepdims=True)
        block = cot_all[s % columns, s // columns]
        picked = jnp.dot(hit.astype(BF), block, preferred_element_type=F32)
        back_ref[s] = (weight * picked).astype(BF)
    for y in range(chips):
        value = jnp.zeros((pair, width), F32)
        for c in range(cores):
            value += transposed_dot(
                hidden_all[y * cores + c].reshape(half_rows, pair),
                back_ref[c * half : (c + 1) * half].reshape(half_rows, width),
            )
        grad_ref[y * pair : (y + 1) * pair, :] = value
    save_grad = pltpu.make_async_copy(grad_ref, grad_hbm, load_sem.at[3])
    save_grad.start()

    for copies in token_rings + cot_rings:
        for copy in copies:
            copy.wait_send()
    for table, kinds in ((tok_all, (TX, TB)), (cot_all, (CX, CB))):
        for kind in kinds:
            remote(table.at[0], table.at[0], kind, sibling).wait_send()
    for copy in token_passed + cot_passed:
        copy.wait_send()
    both = rows_all.at[pl.ds(0, cores)]
    remote(both, both, YU + core, sibling).wait_send()
    remote(both, both, YD + core, sibling).wait_send()
    rows_sibling.wait_send()
    pass_up.wait_send()
    pass_down.wait_send()
    others = hidden_all.at[pl.ds(0, chips - 1)]
    remote(others, others, Y2, sibling).wait_send()
    others = hidden_all.at[pl.ds(0, chips)]
    remote(others, others, Y3, sibling).wait_send()
    for dst, kind in (
        (note_all, SC),
        (down_mid, D1),
        (first_mid, F1),
        (second_mid, S1),
        (down_new, D2),
        (first_new, F2),
        (second_new, S2),
        (hid_mid, H1),
        (hid_new, H2),
        (out_recv, O),
    ):
        sent_all(dst, kind)
    wait_all(first_out, first_new, F2)
    wait_all(second_out, second_new, S2)
    wait_all(out_send, out_recv, O)
    for save in (save_down, save_pick, save_wide, save_grad):
        save.wait()


def finish_kernel(
    grad_hbm,
    down_hbm,
    first_hbm,
    second_hbm,
    wide_hbm,
    pick_hbm,
    rows_hbm,
    mixed_hbm,
    fresh_hbm,
    first_out,
    second_out,
    grad_ref,
    state_ref,
    wide_ref,
    pick_ref,
    rows_ref,
    mixed_ref,
    fresh_ref,
    first_ref,
    second_ref,
    load_sem,
    store_sem,
    other_sem,
):
    total, width = grad_ref.shape
    tall = QB
    chunks = total // tall
    pieces = tall // state_ref.shape[2]
    others = [
        pltpu.make_async_copy(src, dst, other_sem.at[k])
        for k, (src, dst) in enumerate(
            [(wide_hbm, wide_ref), (pick_hbm, pick_ref), (rows_hbm, rows_ref)]
        )
    ]
    others[0].start()
    loads = []
    for r in range(chunks):
        rows = pl.ds(r * tall, tall)
        block = pl.ds(r * pieces, pieces)
        copies = [pltpu.make_async_copy(grad_hbm.at[rows], grad_ref.at[rows], load_sem.at[r, 0])]
        for k, src in enumerate((down_hbm, first_hbm, second_hbm)):
            copies.append(
                pltpu.make_async_copy(
                    src.at[block], state_ref.at[k, block], load_sem.at[r, k + 1]
                )
            )
        for copy in copies:
            copy.start()
        loads.append(copies)
    others[1].start()
    others[2].start()
    others[0].wait()
    stores = []
    for r in range(chunks):
        for copy in loads[r]:
            copy.wait()
        rows = pl.ds(r * tall, tall)
        block = pl.ds(r * pieces, pieces)
        grad = grad_ref[rows, :]
        quant = state_ref[0, block].reshape(tall, width).astype(F32)
        master = quant * wide_ref[r : r + 1, :]
        first = state_ref[1, block].reshape(tall, width).astype(F32)
        second = state_ref[2, block].reshape(tall, width).astype(F32)
        first = beta_first * first + (1.0 - beta_first) * grad
        second = beta_second * second + (1.0 - beta_second) * grad * grad
        size = jnp.sqrt(second * (1.0 / fix_second)) + adam_eps
        update = first * (1.0 / fix_first) / size
        first_ref[rows, :] = first
        second_ref[rows, :] = second
        fresh_ref[rows, :] = (master - learn_rate * (update + decay_rate * master)).astype(BF)
        for k, (src, dst) in enumerate(
            ((first_ref, first_out), (second_ref, second_out), (fresh_ref, fresh_hbm))
        ):
            store = pltpu.make_async_copy(src.at[rows], dst.at[0, rows], store_sem.at[r, k])
            store.start()
            stores.append(store)
    others[1].wait()
    others[2].wait()
    returned = rows_ref[...].reshape(-1, width)
    value = transposed_dot(pick_ref[0], returned)
    value += transposed_dot(pick_ref[1], returned)
    mixed_ref[...] = value.astype(BF)
    store = pltpu.make_async_copy(mixed_ref, mixed_hbm, other_sem.at[3])
    store.start()
    stores.append(store)
    for store in stores:
        store.wait()


def finish(grad, down_new, first_new, second_new, wide, pick, out_rows):
    hidden_total, width = grad.shape
    tokens = pick.shape[2]
    chunks = hidden_total // QB
    hbm = pl.BlockSpec(memory_space=pl.ANY)
    return pl.pallas_call(
        finish_kernel,
        in_specs=[hbm] * 7,
        out_specs=[hbm] * 4,
        out_shape=[
            jax.ShapeDtypeStruct((tokens, width), BF),
            jax.ShapeDtypeStruct((1, hidden_total, width), BF),
            jax.ShapeDtypeStruct((1, hidden_total, width), F32),
            jax.ShapeDtypeStruct((1, hidden_total, width), F32),
        ],
        scratch_shapes=[
            pltpu.VMEM((hidden_total, width), F32),
            pltpu.VMEM((3,) + down_new.shape, BF),
            pltpu.VMEM(wide.shape, F32),
            pltpu.VMEM(pick.shape, BF),
            pltpu.VMEM(out_rows.shape, BF),
            pltpu.VMEM((tokens, width), BF),
            pltpu.VMEM((hidden_total, width), BF),
            pltpu.VMEM((hidden_total, width), F32),
            pltpu.VMEM((hidden_total, width), F32),
            pltpu.SemaphoreType.DMA((chunks, 4)),
            pltpu.SemaphoreType.DMA((chunks, 3)),
            pltpu.SemaphoreType.DMA((4,)),
        ],
        compiler_params=pltpu.CompilerParams(vmem_limit_bytes=VMEM_LIMIT),
        name="finish",
    )(grad, down_new, first_new, second_new, wide, pick, out_rows)


def per_device(
    tokens,
    route_weight,
    route_expert,
    cotangent,
    gate_quant,
    up_quant,
    gate_scale,
    up_scale,
    down_quant,
    down_scale,
    first_moment,
    second_moment,
    old_expert,
    new_holder,
):
    number = lax.axis_size("expert")
    parts = lax.axis_size("dp")
    cores = 2
    columns = 4
    tok_rows, top_count = route_expert.shape
    width = cotangent.shape[1]
    slots = min(tok_rows, tok_rows * top_count // number * 4 // 3)
    model_width, hidden_part = gate_quant.shape[1:]
    hidden_total = down_quant.shape[1]
    piece_rows = hidden_total // number
    scale = down_scale[0].T

    hbm = pl.BlockSpec(memory_space=pl.ANY)
    state_shape = (number, piece_rows, width)
    row_shape = (number, slots, width)
    pick_shape = (2, number * slots, tok_rows)
    wide_shape = (hidden_total // QB, width)
    half_rows = number * slots // cores
    state = pltpu.VMEM(state_shape, BF)
    rows = pltpu.VMEM(row_shape, BF)
    note = pltpu.VMEM((number, scale.shape[0], QB), F32)
    hid_shape = (number, half_rows // number, cores * hidden_part)
    hid = pltpu.VMEM(hid_shape, BF)
    parts_out = pl.pallas_call(
        step_kernel,
        in_specs=[hbm] * 14,
        out_specs=[hbm] * 7,
        out_shape=[
            jax.ShapeDtypeStruct((hidden_total, width), F32),
            jax.ShapeDtypeStruct(state_shape, BF),
            jax.ShapeDtypeStruct(state_shape, BF),
            jax.ShapeDtypeStruct(state_shape, BF),
            jax.ShapeDtypeStruct(row_shape, BF),
            jax.ShapeDtypeStruct(pick_shape, BF),
            jax.ShapeDtypeStruct(wide_shape, F32),
        ],
        scratch_shapes=[
            pltpu.SMEM((number,), jnp.int32),
            pltpu.SMEM((number,), jnp.int32),
            pltpu.SMEM((model_width // QB,), F32),
            pltpu.SMEM((model_width // QB,), F32),
            pltpu.VMEM((top_count, tok_rows), jnp.int32),
            pltpu.VMEM((top_count, tok_rows), F32),
            pltpu.VMEM(scale.shape, F32),
            pltpu.VMEM((8, QB), F32),
            pltpu.SMEM((number,), jnp.int32),
            pltpu.VMEM((3, number, QB), F32),
            pltpu.VMEM((columns, number // columns, tok_rows, width), BF),
            rows,
            note,
            note,
            state,
            state,
            state,
            state,
            state,
            pltpu.VMEM((columns, number // columns, tok_rows, width), BF),
            rows,
            state,
            state,
            state,
            state,
            hid,
            hid,
            hid,
            hid,
            rows,
            pltpu.VMEM((parts, number // cores, slots, width), BF),
            pltpu.VMEM((cores, model_width, 2 * hidden_part), BF),
            pltpu.VMEM((model_width, hidden_part), BF),
            pltpu.VMEM((model_width, hidden_part), BF),
            pltpu.VMEM((parts,) + hid_shape, BF),
            pltpu.VMEM((hidden_total, width), F32),
            pltpu.VMEM(pick_shape, BF),
            pltpu.VMEM(wide_shape, F32),
            pltpu.SemaphoreType.DMA((KINDS,)),
            pltpu.SemaphoreType.DMA((KINDS,)),
            pltpu.SemaphoreType.DMA((KINDS,)),
            pltpu.SemaphoreType.DMA((13,)),
        ],
        compiler_params=pltpu.CompilerParams(
            collective_id=0, has_side_effects=True, vmem_limit_bytes=VMEM_LIMIT
        ),
        name="step",
    )(
        old_expert,
        new_holder,
        gate_scale.reshape(-1),
        up_scale.reshape(-1),
        route_expert.T,
        route_weight.T,
        tokens,
        cotangent,
        scale,
        gate_quant[0],
        up_quant[0],
        down_quant.reshape(state_shape),
        first_moment[0],
        second_moment[0],
    )
    grad, down_new, first_new, second_new, out_rows, pick, wide = parts_out
    return tuple(finish(grad, down_new, first_new, second_new, wide, pick, out_rows))


def solution(mesh):
    in_specs = (
        P("expert", "dp"),
        P("expert", None),
        P("expert", None),
        P("expert", "dp"),
        P("expert", None, "dp"),
        P("expert", None, "dp"),
        P("expert", None, "dp"),
        P("expert", None, "dp"),
        P("expert", None, "dp"),
        P("expert", None, "dp"),
        P("expert", None, "dp"),
        P("expert", None, "dp"),
        P(),
        P(),
    )
    out_specs = (
        P("expert", "dp"),
        P("expert", None, "dp"),
        P("expert", None, "dp"),
        P("expert", None, "dp"),
    )
    return jax.shard_map(
        per_device, mesh=mesh, in_specs=in_specs, out_specs=out_specs, check_vma=False
    )
```

```python
import jax
import jax.numpy as jnp
from jax import lax
from jax.experimental import pallas as pl
from jax.experimental.pallas import tpu as pltpu
from jax.sharding import PartitionSpec as P

QB = 128
BF = jnp.bfloat16
F32 = jnp.float32
MESH = pl.DeviceIdType.MESH

beta_first = 0.9
beta_second = 0.95
adam_eps = 1e-08
learn_rate = 0.003
decay_rate = 0.1
step_count = 20
fix_first = 1.0 - beta_first**step_count
fix_second = 1.0 - beta_second**step_count

VMEM_LIMIT = 58 * 1024 * 1024

SC, D1, F1, S1, D2, F2, S2, H1, H2, O, W, CX, TX, YS, YFU, YFD, Y2, Y3 = range(18)
YU = 18
YD = 20
TU = 22
CU = 30
TF = 38
CF = 40
TB = 42
CB = 43
KINDS = 44


def transposed_dot(a, b):
    return lax.dot_general(a, b, (((0,), (0,)), ((), ())), preferred_element_type=F32)


def step_kernel(
    old_hbm,
    holder_hbm,
    gate_scale_hbm,
    up_scale_hbm,
    route_hbm,
    weight_hbm,
    tok_hbm,
    cot_hbm,
    scale_hbm,
    gate_hbm,
    up_hbm,
    down_hbm,
    first_hbm,
    second_hbm,
    grad_hbm,
    down_new_hbm,
    first_new,
    second_new,
    out_recv,
    pick_hbm,
    wide_hbm,
    old_ref,
    holder_ref,
    gate_scale_ref,
    up_scale_ref,
    route_ref,
    weight_ref,
    scale_ref,
    scale_lanes,
    giver_ref,
    lanes_ref,
    tok_all,
    tok_recv,
    note_send,
    note_all,
    down_mid,
    first_send,
    first_mid,
    second_send,
    second_mid,
    cot_all,
    back_ref,
    down_out,
    down_new,
    first_out,
    second_out,
    hid_send,
    hid_mid,
    hid_out,
    hid_new,
    out_send,
    rows_all,
    weights_all,
    gate_v,
    up_v,
    hidden_all,
    grad_ref,
    pick_ref,
    wide_ref,
    send_sem,
    recv_sem,
    local_sem,
    load_sem,
):
    number = lax.axis_size("expert")
    parts = lax.axis_size("dp")
    cores = weights_all.shape[0]
    columns, depth = cot_all.shape[:2]
    e = lax.axis_index("expert")
    d = lax.axis_index("dp")
    core = lax.rem(d, cores)
    z = e // columns
    x = lax.rem(e, columns)
    chip = d // cores
    chips = parts // cores
    tokens, width = tok_all.shape[2:]
    slots = tok_recv.shape[1]
    total = number * slots
    half = number // cores
    half_rows = half * slots
    hidden_part = gate_v.shape[1]

    def remote(src, dst, kind, target):
        return pltpu.make_async_remote_copy(
            src_ref=src,
            dst_ref=dst,
            send_sem=send_sem.at[kind],
            recv_sem=recv_sem.at[kind],
            device_id=target,
            device_id_type=MESH,
        )

    load_gate = pltpu.make_async_copy(gate_hbm, gate_v, load_sem.at[0])
    load_up = pltpu.make_async_copy(up_hbm, up_v, load_sem.at[1])
    load_first = pltpu.make_async_copy(first_hbm, grad_ref, load_sem.at[2])
    load_second = pltpu.make_async_copy(second_hbm, grad_ref, load_sem.at[3])
    small = [
        pltpu.make_async_copy(src, dst, load_sem.at[4 + i])
        for i, (src, dst) in enumerate(
            [
                (route_hbm, route_ref),
                (old_hbm, old_ref),
                (tok_hbm, tok_all.at[x, z]),
                (cot_hbm, cot_all.at[x, z]),
                (weight_hbm, weight_ref),
                (holder_hbm, holder_ref),
                (gate_scale_hbm, gate_scale_ref),
                (up_scale_hbm, up_scale_ref),
                (scale_hbm, scale_ref),
            ]
        )
    ]
    for load in small:
        load.start()
    load_gate.start()
    load_up.start()
    load_first.start()

    barrier = pltpu.get_barrier_semaphore()

    def greet_expert(k, carry):
        pl.semaphore_signal(
            barrier, inc=1, device_id=(lax.rem(e + k, number), d), device_id_type=MESH
        )
        return carry

    def greet_dp(k, carry):
        pl.semaphore_signal(
            barrier, inc=1, device_id=(e, lax.rem(d + k, parts)), device_id_type=MESH
        )
        return carry

    lax.fori_loop(1, number, greet_expert, 0)
    lax.fori_loop(1, parts, greet_dp, 0)

    def send_part(src, dst, kind, first, last):
        def body(k, carry):
            t = lax.rem(e + k, number)
            remote(src.at[t], dst.at[e], kind, (t, d)).start()
            return carry

        lax.fori_loop(first, last, body, 0)

    def send_all(src, dst, kind):
        send_part(src, dst, kind, 1, number)
        pltpu.make_async_copy(src.at[e], dst.at[e], local_sem.at[kind]).start()

    def wait_all(src, dst, kind):
        rest = dst.at[pl.ds(0, number - 1)]
        remote(rest, rest, kind, (lax.rem(e + 1, number), d)).wait_recv()
        pltpu.make_async_copy(src.at[e], dst.at[e], local_sem.at[kind]).wait()

    def sent_all(dst, kind):
        rest = dst.at[pl.ds(0, number - 1)]
        remote(rest, rest, kind, (lax.rem(e + 1, number), d)).wait_send()

    def reorder(src, dst):
        def body(k, carry):
            dst[k] = src[giver_ref[k]]
            return carry

        lax.fori_loop(0, number, body, 0)

    def ring(table, base, step):
        above = (lax.rem(z + 1, depth) * columns + x, d)
        below = (lax.rem(z + depth - 1, depth) * columns + x, d)
        from_below = table.at[x, lax.rem(z + depth - step, depth)]
        from_above = table.at[x, lax.rem(z + step, depth)]
        if step == depth // 2 - 1:
            lines = tokens // 2
            from_below = from_below.at[pl.ds(0, lines)]
            from_above = from_above.at[pl.ds(lines, lines)]
        up = remote(from_below, from_below, base + 2 * step, above)
        down = remote(from_above, from_above, base + 2 * step + 1, below)
        return up, down

    sibling = (e, d + 1 - 2 * core)
    right = (z * columns + lax.rem(x + 1, columns), d)
    left = (z * columns + lax.rem(x + columns - 1, columns), d)
    right_x, left_x = lax.rem(x + 1, columns), lax.rem(x + columns - 1, columns)

    def along_x(block, kinds):
        remote(block, block, kinds[0], right).start()
        remote(block, block, kinds[1], left).start()

    def pass_on(table, kinds, onward):
        copies = []
        for kind, k, source, low, target in (
            (kinds[0], onward, left_x, 0, right),
            (kinds[1], onward + 1, right_x, depth // 2, left),
        ):
            column = table.at[source]
            remote(column, column, kind, sibling).wait_recv()
            part = table.at[source, pl.ds(low, depth // 2)]
            copy = remote(part, part, k, target)
            copy.start()
            copies.append(copy)
        return copies

    token_rings = [ring(tok_all, TU, step) for step in range(depth // 2)]
    cot_rings = [ring(cot_all, CU, step) for step in range(depth // 2)]

    def start(copies):
        for copy in copies:
            copy.start()

    def arrive(copies):
        for copy in copies:
            copy.wait_recv()

    small[2].wait()
    pl.semaphore_wait(barrier, number - 1 + parts - 1)

    portion = number // 4
    start(token_rings[0])
    along_x(tok_all.at[x, z], (TX, TB))
    send_part(down_hbm, down_mid, D1, 1, portion)

    i = lax.broadcasted_iota(jnp.int32, (tokens, tokens), 0)
    j = lax.broadcasted_iota(jnp.int32, (tokens, tokens), 1)
    earlier = (i < j).astype(BF)
    label = lax.broadcasted_iota(jnp.int32, (number, tokens), 0)

    def ranks(hit):
        rank = jnp.dot(hit.astype(BF), earlier, preferred_element_type=F32)
        return jnp.where(hit > 0.0, rank, -1.0)

    small[0].wait()
    small[1].wait()
    small[4].wait()
    small[5].wait()
    small[8].wait()
    expert_before = jnp.zeros((number, tokens), jnp.int32)
    expert_after = jnp.zeros((number, tokens), jnp.int32)
    for h in range(number):
        expert_before = jnp.where(label == h, old_ref[h], expert_before)
        expert_after = jnp.where(label == holder_ref[h], old_ref[h], expert_after)
    routes = route_ref[...]
    hit_before = jnp.zeros((number, tokens), F32)
    hit_after = jnp.zeros((number, tokens), F32)
    weight_after = jnp.zeros((number, tokens), F32)
    for k in range(routes.shape[0]):
        hit_before += (routes[k : k + 1, :] == expert_before).astype(F32)
        match = routes[k : k + 1, :] == expert_after
        hit_after += match.astype(F32)
        weight_after += jnp.where(match, weight_ref[k : k + 1, :], 0.0)
    rank_after = ranks(hit_after)
    lanes_ref[...] = jnp.zeros_like(lanes_ref)
    lanes_ref[0, :, :tokens] = rank_after
    lanes_ref[1, :, :tokens] = weight_after
    lanes_ref[2, :, :tokens] = ranks(hit_before)
    scale_lanes[...] = jnp.zeros_like(scale_lanes)
    scale_lanes[: scale_ref.shape[0], : scale_ref.shape[1]] = scale_ref[...]
    scale_note = pltpu.roll(scale_lanes[...], tokens, 1)[: scale_ref.shape[0], :]
    note_shape = note_send.shape[1:]
    line = lax.broadcasted_iota(jnp.int32, note_shape, 0)
    lane = lax.broadcasted_iota(jnp.int32, note_shape, 1)
    for h in range(number):
        note = jnp.zeros(note_shape, F32)
        for r in range(3):
            spread_row = jnp.broadcast_to(lanes_ref[r, h : h + 1, :], note_shape)
            note = jnp.where(line == r, spread_row, note)
        note_send[h] = jnp.where(lane < tokens, note, scale_note)
    send_all(note_send, note_all, SC)

    def ring_step(table, rings, step, kind):
        arrive(rings[step - 1])
        start(rings[step])
        along_x(table.at[x, lax.rem(z + depth - step, depth)], kind)
        along_x(table.at[x, lax.rem(z + step, depth)], kind)

    def ring_end(table, rings, kind):
        arrive(rings[-1])
        along_x(table.at[x, lax.rem(z + depth // 2, depth)], kind)

    ring_step(tok_all, token_rings, 1, (TX, TB))
    send_part(down_hbm, down_mid, D1, portion, 2 * portion)
    ring_step(tok_all, token_rings, 2, (TX, TB))
    send_part(down_hbm, down_mid, D1, 2 * portion, 3 * portion)
    ring_step(tok_all, token_rings, 3, (TX, TB))
    send_part(down_hbm, down_mid, D1, 3 * portion, number)
    pltpu.make_async_copy(down_hbm.at[e], down_mid.at[e], local_sem.at[D1]).start()

    load_first.wait()
    first_send[...] = grad_ref[...].astype(BF).reshape(first_send.shape)
    load_second.start()

    ring_end(tok_all, token_rings, (TX, TB))
    small[3].wait()
    start(cot_rings[0])
    send_all(first_send, first_mid, F1)

    load_gate.wait()
    load_up.wait()
    small[6].wait()
    small[7].wait()

    def dequantize(r, carry):
        lines = pl.ds(pl.multiple_of(r * QB, QB), QB)
        gate = (gate_v[lines, :].astype(F32) * gate_scale_ref[r]).astype(BF)
        up = (up_v[lines, :].astype(F32) * up_scale_ref[r]).astype(BF)
        weights_all[core, lines, :] = jnp.concatenate([gate, up], axis=1)
        return carry

    lax.fori_loop(0, gate_v.shape[0] // QB, dequantize, 0)
    weights_copy = remote(weights_all.at[core], weights_all.at[core], W, sibling)
    weights_copy.start()

    def find(h, carry):
        giver = jnp.int32(0)
        for g in range(number):
            giver = jnp.where(holder_ref[g] == h, g, giver)
        giver_ref[h] = giver
        return carry

    lax.fori_loop(0, number, find, 0)

    token_passed = pass_on(tok_all, (TX, TB), TF)
    wait_all(note_send, note_all, SC)
    for copy in token_passed:
        copy.wait_recv()
    slot = lax.broadcasted_iota(jnp.int32, (slots, tokens), 0).astype(F32)
    for s in range(number):
        hit = (note_all[s, 2:3, :tokens] == slot).astype(BF)
        block = tok_all[s % columns, s // columns]
        tok_recv[s] = jnp.dot(hit, block, preferred_element_type=F32).astype(BF)

    up_chip = lax.rem(chip + 1, chips) * cores
    down_chip = lax.rem(chip + chips - 1, chips) * cores
    for c in range(cores):
        src = tok_recv.at[pl.ds(c * half, half)]
        remote(src, rows_all.at[d], YU + core, (e, up_chip + c)).start()
        remote(src, rows_all.at[d], YD + core, (e, down_chip + c)).start()
    rows_sibling = remote(
        tok_recv.at[pl.ds((1 - core) * half, half)], rows_all.at[d], YS, sibling
    )
    rows_sibling.start()

    load_second.wait()
    second_send[...] = grad_ref[...].astype(BF).reshape(second_send.shape)
    arrive(cot_rings[0])
    start(cot_rings[1])
    send_all(second_send, second_mid, S1)
    wait_all(down_hbm, down_mid, D1)
    reorder(down_mid, down_out)
    send_all(down_out, down_new, D2)

    def row_chunk(k):
        return rows_all.at[k]

    def arrived(kind, k):
        remote(row_chunk(k), row_chunk(k), kind, sibling).wait_recv()

    arrived(YU, down_chip)
    pass_up = remote(row_chunk(down_chip), row_chunk(down_chip), YFU, (e, up_chip + core))
    pass_up.start()
    arrived(YD + 1, up_chip + 1)
    pass_down = remote(
        row_chunk(up_chip + 1), row_chunk(up_chip + 1), YFD, (e, down_chip + core)
    )
    pass_down.start()
    arrive(cot_rings[1])
    start(cot_rings[2])
    arrive(cot_rings[2])
    start(cot_rings[3])

    rows_sibling.wait_recv()
    weights_copy.wait()
    arrived(YU + 1, down_chip + 1)
    arrived(YD, up_chip)
    far_chip = lax.rem(chip + 2, chips) * cores

    def partial(chunk, values):
        lines = pl.ds(pl.multiple_of(chunk * width, width), width)
        return [
            value
            + jnp.dot(chunk_rows, weights_all[c, lines, :], preferred_element_type=F32)
            for c, value in enumerate(values)
        ]

    values = [jnp.zeros((half_rows, 2 * hidden_part), F32) for _ in range(cores)]
    own = tok_recv[pl.ds(core * half, half)].reshape(half_rows, width)
    for chunk in (
        d,
        d + 1 - 2 * core,
        down_chip,
        down_chip + 1,
        up_chip,
        up_chip + 1,
        far_chip,
        far_chip + 1,
    ):
        if chunk is d:
            chunk_rows = own
        else:
            if chunk is far_chip:
                arrived(YFU, far_chip)
                arrived(YFD, far_chip + 1)
            chunk_rows = rows_all[chunk].reshape(half_rows, width)
        values = partial(chunk, values)
    for c, value in enumerate(values):
        gate = value[:, :hidden_part]
        up = value[:, hidden_part:]
        act = (gate / (1.0 + jnp.exp(-gate)) * up).astype(BF)
        hid_send[:, :, c * hidden_part : (c + 1) * hidden_part] = act.reshape(
            number, half_rows // number, hidden_part
        )
    send_all(hid_send, hid_mid, H1)
    wait_all(first_send, first_mid, F1)
    reorder(first_mid, first_out)
    send_part(first_out, first_new, F2, 1, number // 2)
    arrive(cot_rings[-1])
    along_x(cot_all.at[x], (CX, CB))


    wait_all(hid_send, hid_mid, H1)
    reorder(hid_mid, hid_out)
    send_all(hid_out, hid_new, H2)
    send_part(first_out, first_new, F2, number // 2, number)
    pltpu.make_async_copy(first_out.at[e], first_new.at[e], local_sem.at[F2]).start()
    wait_all(second_send, second_mid, S1)
    reorder(second_mid, second_out)
    send_all(second_out, second_new, S2)


    row = lax.broadcasted_iota(jnp.int32, (total, number), 0)
    holder = lax.broadcasted_iota(jnp.int32, (total, number), 1)
    spread = jnp.logical_and(row >= holder * slots, row < (holder + 1) * slots).astype(BF)
    place = lax.rem(lax.broadcasted_iota(jnp.int32, (total, tokens), 0), slots).astype(F32)
    wide_rank = jnp.dot(
        spread, lanes_ref[0, :, :tokens].astype(BF), preferred_element_type=F32
    )
    hit_slots = wide_rank == place
    rest = lanes_ref[1, :, :tokens]
    for p in range(pick_ref.shape[0]):
        piece = rest.astype(BF)
        rest = rest - piece.astype(F32)
        wide = jnp.dot(spread, piece, preferred_element_type=F32)
        pick_ref[p] = jnp.where(hit_slots, wide, 0.0).astype(BF)
    save_pick = pltpu.make_async_copy(pick_ref, pick_hbm, load_sem.at[1])
    save_pick.start()

    wait_all(hid_out, hid_new, H2)

    own_hidden = pltpu.make_async_copy(hid_new, hidden_all.at[d], local_sem.at[Y2])
    own_hidden.start()
    for k in range(1, chips):
        target = lax.rem(chip + k, chips) * cores + core
        remote(hid_new, hidden_all.at[d], Y2, (e, target)).start()
    remote(hid_new, hidden_all.at[d], Y3, sibling).start()

    others = hidden_all.at[pl.ds(0, chips - 1)]
    remote(others, others, Y2, sibling).wait_recv()
    for k in range(1, chips):
        chunk = hidden_all.at[lax.rem(chip + k, chips) * cores + core]
        remote(chunk, chunk, Y3, sibling).start()

    cot_passed = pass_on(cot_all, (CX, CB), CF)
    wait_all(down_out, down_new, D2)
    save_down = pltpu.make_async_copy(down_new, down_new_hbm, load_sem.at[0])
    save_down.start()
    scale = note_all[giver_ref[e]]
    scale_wide = jnp.concatenate(
        [
            jnp.concatenate(
                [
                    jnp.broadcast_to(scale[c : c + 1, tokens + r : tokens + r + 1], (1, QB))
                    for c in range(width // QB)
                ],
                axis=1,
            )
            for r in range(wide_ref.shape[0])
        ],
        axis=0,
    )
    wide_ref[...] = scale_wide
    save_wide = pltpu.make_async_copy(wide_ref, wide_hbm, load_sem.at[2])
    save_wide.start()
    pieces = QB // down_new.shape[1]

    def weight_rows(r):
        quant = down_new[r * pieces : (r + 1) * pieces].reshape(QB, width)
        return (quant.astype(F32) * scale_wide[r : r + 1, :]).astype(BF)

    own_hidden.wait()
    others = hidden_all.at[pl.ds(0, chips)]
    remote(others, others, Y3, sibling).wait_recv()
    pair = cores * hidden_part
    for c in range(cores):
        value = jnp.zeros((half_rows, width), F32)
        for y in range(chips):
            down_w = jnp.concatenate(
                [weight_rows(y * pair // QB + r) for r in range(pair // QB)], axis=0
            )
            value += jnp.dot(
                hidden_all[y * cores + c].reshape(half_rows, pair),
                down_w,
                preferred_element_type=F32,
            )
        out_send[c * half : (c + 1) * half] = value.astype(BF).reshape(half, slots, width)

        def send_half(k, carry, c=c):
            t = c * half + lax.rem(e + k, half)

            @pl.when(t != e)
            def _():
                remote(out_send.at[t], out_recv.at[e], O, (t, d)).start()

            return carry

        lax.fori_loop(0, half, send_half, 0)
    pltpu.make_async_copy(out_send.at[e], out_recv.at[e], local_sem.at[O]).start()

    for copy in cot_passed:
        copy.wait_recv()
    for s in range(number):
        hit = note_all[s, 0:1, :tokens] == slot
        weight = jnp.sum(jnp.where(hit, note_all[s, 1:2, :tokens], 0.0), axis=1, keepdims=True)
        block = cot_all[s % columns, s // columns]
        picked = jnp.dot(hit.astype(BF), block, preferred_element_type=F32)
        back_ref[s] = (weight * picked).astype(BF)
    for y in range(chips):
        value = jnp.zeros((pair, width), F32)
        for c in range(cores):
            value += transposed_dot(
                hidden_all[y * cores + c].reshape(half_rows, pair),
                back_ref[c * half : (c + 1) * half].reshape(half_rows, width),
            )
        grad_ref[y * pair : (y + 1) * pair, :] = value
    save_grad = pltpu.make_async_copy(grad_ref, grad_hbm, load_sem.at[3])
    save_grad.start()

    for copies in token_rings + cot_rings:
        for copy in copies:
            copy.wait_send()
    for table, kinds in ((tok_all, (TX, TB)), (cot_all, (CX, CB))):
        for kind in kinds:
            remote(table.at[0], table.at[0], kind, sibling).wait_send()
    for copy in token_passed + cot_passed:
        copy.wait_send()
    both = rows_all.at[pl.ds(0, cores)]
    remote(both, both, YU + core, sibling).wait_send()
    remote(both, both, YD + core, sibling).wait_send()
    rows_sibling.wait_send()
    pass_up.wait_send()
    pass_down.wait_send()
    others = hidden_all.at[pl.ds(0, chips - 1)]
    remote(others, others, Y2, sibling).wait_send()
    others = hidden_all.at[pl.ds(0, chips)]
    remote(others, others, Y3, sibling).wait_send()
    for dst, kind in (
        (note_all, SC),
        (down_mid, D1),
        (first_mid, F1),
        (second_mid, S1),
        (down_new, D2),
        (first_new, F2),
        (second_new, S2),
        (hid_mid, H1),
        (hid_new, H2),
        (out_recv, O),
    ):
        sent_all(dst, kind)
    wait_all(first_out, first_new, F2)
    wait_all(second_out, second_new, S2)
    wait_all(out_send, out_recv, O)
    for save in (save_down, save_pick, save_wide, save_grad):
        save.wait()


def finish_kernel(
    grad_hbm,
    down_hbm,
    first_hbm,
    second_hbm,
    wide_hbm,
    pick_hbm,
    rows_hbm,
    mixed_hbm,
    fresh_hbm,
    first_out,
    second_out,
    grad_ref,
    state_ref,
    wide_ref,
    pick_ref,
    rows_ref,
    mixed_ref,
    fresh_ref,
    first_ref,
    second_ref,
    load_sem,
    store_sem,
    other_sem,
):
    total, width = grad_ref.shape
    tall = 2 * QB
    chunks = total // tall
    pieces = tall // state_ref.shape[2]
    others = [
        pltpu.make_async_copy(src, dst, other_sem.at[k])
        for k, (src, dst) in enumerate(
            [(wide_hbm, wide_ref), (pick_hbm, pick_ref), (rows_hbm, rows_ref)]
        )
    ]
    others[0].start()
    loads = []
    for r in range(chunks):
        rows = pl.ds(r * tall, tall)
        block = pl.ds(r * pieces, pieces)
        copies = [pltpu.make_async_copy(grad_hbm.at[rows], grad_ref.at[rows], load_sem.at[r, 0])]
        for k, src in enumerate((down_hbm, first_hbm, second_hbm)):
            copies.append(
                pltpu.make_async_copy(
                    src.at[block], state_ref.at[k, block], load_sem.at[r, k + 1]
                )
            )
        for copy in copies:
            copy.start()
        loads.append(copies)
    others[1].start()
    others[2].start()
    others[0].wait()
    stores = []
    for r in range(chunks):
        for copy in loads[r]:
            copy.wait()
        rows = pl.ds(r * tall, tall)
        block = pl.ds(r * pieces, pieces)
        grad = grad_ref[rows, :]
        quant = state_ref[0, block].reshape(tall, width).astype(F32)
        master = jnp.concatenate(
            [
                quant[:QB, :] * wide_ref[2 * r : 2 * r + 1, :],
                quant[QB:, :] * wide_ref[2 * r + 1 : 2 * r + 2, :],
            ],
            axis=0,
        )
        first = state_ref[1, block].reshape(tall, width).astype(F32)
        second = state_ref[2, block].reshape(tall, width).astype(F32)
        first = beta_first * first + (1.0 - beta_first) * grad
        second = beta_second * second + (1.0 - beta_second) * grad * grad
        size = jnp.sqrt(second * (1.0 / fix_second)) + adam_eps
        update = first * (1.0 / fix_first) / size
        first_ref[rows, :] = first
        second_ref[rows, :] = second
        fresh_ref[rows, :] = (master - learn_rate * (update + decay_rate * master)).astype(BF)
        for k, (src, dst) in enumerate(
            ((first_ref, first_out), (second_ref, second_out), (fresh_ref, fresh_hbm))
        ):
            store = pltpu.make_async_copy(src.at[rows], dst.at[0, rows], store_sem.at[r, k])
            store.start()
            stores.append(store)
    others[1].wait()
    others[2].wait()
    returned = rows_ref[...].reshape(-1, width)
    value = transposed_dot(pick_ref[0], returned)
    value += transposed_dot(pick_ref[1], returned)
    mixed_ref[...] = value.astype(BF)
    store = pltpu.make_async_copy(mixed_ref, mixed_hbm, other_sem.at[3])
    store.start()
    stores.append(store)
    for store in stores:
        store.wait()


def finish(grad, down_new, first_new, second_new, wide, pick, out_rows):
    hidden_total, width = grad.shape
    tokens = pick.shape[2]
    chunks = hidden_total // (2 * QB)
    hbm = pl.BlockSpec(memory_space=pl.ANY)
    return pl.pallas_call(
        finish_kernel,
        in_specs=[hbm] * 7,
        out_specs=[hbm] * 4,
        out_shape=[
            jax.ShapeDtypeStruct((tokens, width), BF),
            jax.ShapeDtypeStruct((1, hidden_total, width), BF),
            jax.ShapeDtypeStruct((1, hidden_total, width), F32),
            jax.ShapeDtypeStruct((1, hidden_total, width), F32),
        ],
        scratch_shapes=[
            pltpu.VMEM((hidden_total, width), F32),
            pltpu.VMEM((3,) + down_new.shape, BF),
            pltpu.VMEM(wide.shape, F32),
            pltpu.VMEM(pick.shape, BF),
            pltpu.VMEM(out_rows.shape, BF),
            pltpu.VMEM((tokens, width), BF),
            pltpu.VMEM((hidden_total, width), BF),
            pltpu.VMEM((hidden_total, width), F32),
            pltpu.VMEM((hidden_total, width), F32),
            pltpu.SemaphoreType.DMA((chunks, 4)),
            pltpu.SemaphoreType.DMA((chunks, 3)),
            pltpu.SemaphoreType.DMA((4,)),
        ],
        compiler_params=pltpu.CompilerParams(vmem_limit_bytes=VMEM_LIMIT),
        name="finish",
    )(grad, down_new, first_new, second_new, wide, pick, out_rows)


def per_device(
    tokens,
    route_weight,
    route_expert,
    cotangent,
    gate_quant,
    up_quant,
    gate_scale,
    up_scale,
    down_quant,
    down_scale,
    first_moment,
    second_moment,
    old_expert,
    new_holder,
):
    number = lax.axis_size("expert")
    parts = lax.axis_size("dp")
    cores = 2
    columns = 4
    tok_rows, top_count = route_expert.shape
    width = cotangent.shape[1]
    slots = min(tok_rows, tok_rows * top_count // number * 4 // 3)
    model_width, hidden_part = gate_quant.shape[1:]
    hidden_total = down_quant.shape[1]
    piece_rows = hidden_total // number
    scale = down_scale[0].T

    hbm = pl.BlockSpec(memory_space=pl.ANY)
    state_shape = (number, piece_rows, width)
    row_shape = (number, slots, width)
    pick_shape = (2, number * slots, tok_rows)
    wide_shape = (hidden_total // QB, width)
    half_rows = number * slots // cores
    state = pltpu.VMEM(state_shape, BF)
    rows = pltpu.VMEM(row_shape, BF)
    note = pltpu.VMEM((number, scale.shape[0], QB), F32)
    hid_shape = (number, half_rows // number, cores * hidden_part)
    hid = pltpu.VMEM(hid_shape, BF)
    parts_out = pl.pallas_call(
        step_kernel,
        in_specs=[hbm] * 14,
        out_specs=[hbm] * 7,
        out_shape=[
            jax.ShapeDtypeStruct((hidden_total, width), F32),
            jax.ShapeDtypeStruct(state_shape, BF),
            jax.ShapeDtypeStruct(state_shape, BF),
            jax.ShapeDtypeStruct(state_shape, BF),
            jax.ShapeDtypeStruct(row_shape, BF),
            jax.ShapeDtypeStruct(pick_shape, BF),
            jax.ShapeDtypeStruct(wide_shape, F32),
        ],
        scratch_shapes=[
            pltpu.SMEM((number,), jnp.int32),
            pltpu.SMEM((number,), jnp.int32),
            pltpu.SMEM((model_width // QB,), F32),
            pltpu.SMEM((model_width // QB,), F32),
            pltpu.VMEM((top_count, tok_rows), jnp.int32),
            pltpu.VMEM((top_count, tok_rows), F32),
            pltpu.VMEM(scale.shape, F32),
            pltpu.VMEM((8, QB), F32),
            pltpu.SMEM((number,), jnp.int32),
            pltpu.VMEM((3, number, QB), F32),
            pltpu.VMEM((columns, number // columns, tok_rows, width), BF),
            rows,
            note,
            note,
            state,
            state,
            state,
            state,
            state,
            pltpu.VMEM((columns, number // columns, tok_rows, width), BF),
            rows,
            state,
            state,
            state,
            state,
            hid,
            hid,
            hid,
            hid,
            rows,
            pltpu.VMEM((parts, number // cores, slots, width), BF),
            pltpu.VMEM((cores, model_width, 2 * hidden_part), BF),
            pltpu.VMEM((model_width, hidden_part), BF),
            pltpu.VMEM((model_width, hidden_part), BF),
            pltpu.VMEM((parts,) + hid_shape, BF),
            pltpu.VMEM((hidden_total, width), F32),
            pltpu.VMEM(pick_shape, BF),
            pltpu.VMEM(wide_shape, F32),
            pltpu.SemaphoreType.DMA((KINDS,)),
            pltpu.SemaphoreType.DMA((KINDS,)),
            pltpu.SemaphoreType.DMA((KINDS,)),
            pltpu.SemaphoreType.DMA((13,)),
        ],
        compiler_params=pltpu.CompilerParams(
            collective_id=0, has_side_effects=True, vmem_limit_bytes=VMEM_LIMIT
        ),
        name="step",
    )(
        old_expert,
        new_holder,
        gate_scale.reshape(-1),
        up_scale.reshape(-1),
        route_expert.T,
        route_weight.T,
        tokens,
        cotangent,
        scale,
        gate_quant[0],
        up_quant[0],
        down_quant.reshape(state_shape),
        first_moment[0],
        second_moment[0],
    )
    grad, down_new, first_new, second_new, out_rows, pick, wide = parts_out
    return tuple(finish(grad, down_new, first_new, second_new, wide, pick, out_rows))


def solution(mesh):
    in_specs = (
        P("expert", "dp"),
        P("expert", None),
        P("expert", None),
        P("expert", "dp"),
        P("expert", None, "dp"),
        P("expert", None, "dp"),
        P("expert", None, "dp"),
        P("expert", None, "dp"),
        P("expert", None, "dp"),
        P("expert", None, "dp"),
        P("expert", None, "dp"),
        P("expert", None, "dp"),
        P(),
        P(),
    )
    out_specs = (
        P("expert", "dp"),
        P("expert", None, "dp"),
        P("expert", None, "dp"),
        P("expert", None, "dp"),
    )
    return jax.shard_map(
        per_device, mesh=mesh, in_specs=in_specs, out_specs=out_specs, check_vma=False
    )
```
